32 devices in a mesh: groups: 2 (over y), dp: 4 (over x, core), tensor: 4 (over z).
Axes of the slice: x: 2, y: 2, z: 4, core: 2. Of those that a mesh axis runs over, the one named last changes fastest.
Arguments:
- tokens: bfloat16 [6144, 8192], P(('groups', 'dp'), 'tensor'), parts along dimension 0, may hold values from -6 to 6
- query_base_weight: bfloat16 [8192, 8192], P(None, 'tensor'), may hold values from -0.0625 to 0.0625
- stored_shrink_factors: bfloat16 [1024, 16, 8192], P('dp', None, 'tensor'), may hold values from -0.0625 to 0.0625
- stored_expand_factors: bfloat16 [1024, 16, 8192], P('dp', None, 'tensor'), may hold values from -1.5 to 1.5
- segment_adapter: int32 [8, 64], P('groups'), parts along dimension 0, may hold values from 0 to 1023, as said below
- segment_length: int32 [8, 64], P(('groups', 'dp')), parts along dimension 0, may hold values from 1 to 48, 768 in all within a row
- adapter_storage_slot: int32 [2048], P('groups'), parts along dimension 0, may hold values from 0 to 1023, as said below
Outputs:
- queries: bfloat16 [6144, 8192], P(('groups', 'dp'), 'tensor'), parts along dimension 0
The draws below stay inside these ranges and needn't reach their ends.
There are 2 independent parts, one for each index of `groups`. The reference program is written for one: setup_inputs(seed, part) draws one part's arguments, and reference() takes and returns one part's arrays. A program takes and returns all parts, laid end to end along the dimension named above; an argument that names none is the same for every part. Nothing has to cross between parts.
Inputs may be any that keep to these rules, and one draw needn't show every extreme that they name: `segment_adapter`: each dp group's 64 segments name distinct adapters; in every group exactly 32 of them have one home dp group, and no home holds more than 32 of one group's adapters. `adapter_storage_slot`: A permutation of the slots. `segment_length`: each row sums to 768.
All inputs are finite; a program needn't handle non-finite values.
Results may differ from the reference program's by a relative error of at most 0.004.
Values may be sent and summed in bfloat16 or wider, within the bound.
No kernel may reach another device: no remote copies, remote signals or barrier semaphores. Data moves between devices by JAX's collectives and lax.ppermute only.
A program may use at most 320 MiB of HBM per device.

```python
import math
import jax
import jax.numpy as jnp
import numpy as np
from jax import lax

MODEL_WIDTH = 8192
QUERY_WIDTH = 8192
ADAPTER_RANK = 16
R_DEV = 768
USED = 64
MOST = 48
ADP_DEV = 256
ADAPTER_TOTAL = 1024
REQUESTS = 3072
N_DP = 4


def adapter_tables(key):
    k_perm, k_hot, k_rest, k_local, k_order = jax.random.split(key, 5)
    groups = ADAPTER_TOTAL // ADP_DEV
    cap = USED // 2
    slot_of = jax.random.permutation(k_perm, ADAPTER_TOTAL)
    adapter_at = jnp.argsort(slot_of)
    hot = jax.random.randint(k_hot, (groups,), 0, groups)
    rest = (hot[:, None] + jax.random.randint(k_rest, (groups, USED - cap), 1, groups)) % groups
    homes = jnp.concatenate([jnp.broadcast_to(hot[:, None], (groups, cap)), rest], axis=1)
    count = USED - cap
    same = rest[:, :, None] == rest[:, None, :]
    earlier = jnp.arange(count)[None, :] < jnp.arange(count)[:, None]
    rank_rest = jnp.sum(jnp.where(same & earlier[None], 1, 0), axis=2)
    ranks = jnp.concatenate([jnp.broadcast_to(jnp.arange(cap)[None, :], (groups, cap)), rank_rest], axis=1)
    local_perm = jax.vmap(lambda k: jax.random.permutation(k, ADP_DEV))(jax.random.split(k_local, groups))
    local = jnp.take_along_axis(local_perm, ranks, axis=1)
    adapters = adapter_at[homes * ADP_DEV + local]
    order = jax.vmap(lambda k: jax.random.permutation(k, USED))(jax.random.split(k_order, groups))
    adapters = jnp.take_along_axis(adapters, order, axis=1)
    return (slot_of.astype(jnp.int32), adapters.astype(jnp.int32))


def draw_segment_adapter(key, part):
    return adapter_tables(key)[1]


def draw_adapter_storage_slot(key, part):
    return adapter_tables(key)[0]


def levels(own_key, extent, shards, smallest, largest):
    factor_of, own = 1.0, jax.random.fold_in(own_key, 6)
    for position, parts in shards:
        steps = jnp.exp(jax.random.uniform(jax.random.fold_in(own, position), (parts,), jnp.float32, smallest / len(shards), largest / len(shards)))
        factor_of = factor_of * jnp.repeat(steps, extent[position] // parts).reshape([-1 if axis == position else 1 for axis in range(len(extent))])
    return factor_of


def split_up(amount, total, reach, lean):
    loads = [(1 << 20) // math.isqrt(grade ** lean) + 1 for grade in range(2, amount + 1)]
    spare, counts = total - reach - (amount - 1), [1] * (amount - 1)
    while spare > 0:
        movable = [i for i in range(amount - 1) if counts[i] < reach]
        whole, left = sum([loads[i] for i in movable]), spare
        for i in movable:
            more = min(reach - counts[i], max(1, left * loads[i] // whole), spare)
            counts[i] = counts[i] + more
            spare = spare - more
    return np.array([reach] + counts)


def ragged(own_key, number_of, total, most, skew):
    if number_of == 2:
        one = jax.random.randint(own_key, (), max(1, total - most), min(most, total - 1) + 1)
        return jnp.stack([one, total - one])
    lengths = jnp.asarray(split_up(number_of, total, most, skew), jnp.int32)
    couples = (number_of - 1) // 2
    donor, taker = lengths[1:1 + 2 * couples:2], lengths[2:2 + 2 * couples:2]
    margin = jnp.minimum(donor - 1, most - taker)
    shifted = jax.random.randint(jax.random.fold_in(own_key, 1), (couples,), 0, 1 << 20) % (margin + 1)
    lengths = lengths.at[1:1 + 2 * couples:2].set(donor - shifted).at[2:2 + 2 * couples:2].set(taker + shifted)
    return lengths[jax.random.permutation(jax.random.fold_in(own_key, 2), number_of)]


def bell_draw(own_key, extent, deviation, limit, shards=(), held_as=jnp.bfloat16):
    factor_of = levels(own_key, extent, shards, -0.22, 0.18) if shards else 1.0
    values = jax.random.normal(own_key, extent, jnp.float32) * deviation * factor_of
    return jnp.minimum(jnp.maximum(values, -limit), limit).astype(held_as)


def setup_inputs(seed: int = 0, part: int = 0) -> dict:
    key_of = jax.random.split(jax.random.key(seed), 8)
    own_keys = jax.random.split(jax.random.fold_in(key_of[7], part), 8)
    tokens = bell_draw(own_keys[0], (REQUESTS, MODEL_WIDTH), 1.0, 6.0, ((0, 4), (1, 4)))
    query_base_weight = bell_draw(key_of[1], (MODEL_WIDTH, QUERY_WIDTH), MODEL_WIDTH ** -0.5, 0.0625, ((1, 4),))
    stored_shrink_factors = bell_draw(key_of[2], (ADAPTER_TOTAL, ADAPTER_RANK, MODEL_WIDTH), MODEL_WIDTH ** -0.5, 0.0625, ((0, 4), (2, 4)))
    stored_expand_factors = bell_draw(key_of[3], (ADAPTER_TOTAL, ADAPTER_RANK, QUERY_WIDTH), ADAPTER_RANK ** -0.5, 1.5, ((0, 4), (2, 4)))
    segment_adapter = draw_segment_adapter(jax.random.fold_in(jax.random.fold_in(key_of[7], part), 71), part)
    segment_length = jax.vmap(lambda own: ragged(own, USED, R_DEV, MOST, 2))(jax.random.split(own_keys[5], N_DP)).reshape((N_DP, USED)).astype(jnp.int32)
    adapter_storage_slot = draw_adapter_storage_slot(jax.random.fold_in(jax.random.fold_in(key_of[7], part), 71), part)
    return {"tokens": tokens, "query_base_weight": query_base_weight, "stored_shrink_factors": stored_shrink_factors, "stored_expand_factors": stored_expand_factors, "segment_adapter": segment_adapter, "segment_length": segment_length, "adapter_storage_slot": adapter_storage_slot}


def reference(tokens, query_base_weight, stored_shrink_factors, stored_expand_factors, segment_adapter, segment_length, adapter_storage_slot):
    base = jnp.dot(tokens, query_base_weight, preferred_element_type=jnp.float32)
    seg_slot = jnp.take(adapter_storage_slot, segment_adapter.reshape(-1)).astype(jnp.int32).reshape(N_DP, USED)
    ends = jnp.cumsum(segment_length, axis=1)
    positions = jnp.arange(R_DEV, dtype=jnp.int32)
    seg_of = jnp.sum((ends[:, None, :] <= positions[None, :, None]).astype(jnp.int32), axis=2).astype(jnp.int32)
    req_slot = jnp.take_along_axis(seg_slot, seg_of, axis=1).reshape(-1).astype(jnp.int32)
    block = math.gcd(REQUESTS, 128)

    def one_block(lookup_index):
        start = (lookup_index * block).astype(jnp.int32)
        rows = lax.dynamic_slice_in_dim(tokens, start, block, 0).astype(jnp.float32)
        storage_slots = lax.dynamic_slice_in_dim(req_slot, start, block, 0)
        shrink_factor = jnp.take(stored_shrink_factors, storage_slots, axis=0).astype(jnp.float32)
        shrink = jnp.einsum("rd,rkd->rk", rows, shrink_factor)
        shrink_low = shrink.astype(jnp.bfloat16).astype(jnp.float32)
        expand_factor = jnp.take(stored_expand_factors, storage_slots, axis=0).astype(jnp.float32)
        return jnp.einsum("rk,rkq->rq", shrink_low, expand_factor)

    expand = lax.map(one_block, jnp.arange(REQUESTS // block, dtype=jnp.int32))
    expand = expand.reshape(REQUESTS, QUERY_WIDTH)
    return (base + expand).astype(jnp.bfloat16)
```

```python
import functools

import jax
import jax.numpy as jnp
from jax import lax
from jax.experimental import pallas as pl
from jax.experimental.pallas import tpu as pltpu
from jax.sharding import PartitionSpec as P

F32 = jnp.float32
BF16 = jnp.bfloat16
ROOM = 48 * 1024 * 1024
TILE = 512


class Order:
    def __init__(self, first):
        self.last = first

    def call(self, kernel, at, args, specs, waits=(), **rest):
        after = [] if rest.get("input_output_aliases") else [self.last]
        after += waits

        def body(at_ref, *refs):
            kernel(at_ref, *refs[: len(args)], *refs[len(args) + len(after) :])

        outs = pl.pallas_call(
            body,
            grid_spec=pltpu.PrefetchScalarGridSpec(
                num_scalar_prefetch=1,
                in_specs=list(specs) + [pl.BlockSpec(memory_space=pl.ANY)] * len(after),
                **rest.pop("grid_spec"),
            ),
            compiler_params=pltpu.CompilerParams(vmem_limit_bytes=ROOM),
            cost_estimate=pl.CostEstimate(flops=1, bytes_accessed=1, transcendentals=0),
            **rest,
        )(at, *args, *after)
        self.last = outs[0] if isinstance(outs, (list, tuple)) else outs
        return outs


    def hold(self, x):
        self.last = pl.pallas_call(
            lambda *_: None,
            out_shape=jax.ShapeDtypeStruct(x.shape, x.dtype),
            in_specs=[pl.BlockSpec(memory_space=pl.ANY)] * 2,
            out_specs=pl.BlockSpec(memory_space=pl.ANY),
            input_output_aliases={0: 0},
            cost_estimate=pl.CostEstimate(flops=1, bytes_accessed=1, transcendentals=0),
        )(x, self.last)
        return self.last


def fetch_kernel(lists_ref, *refs, stores, plan):
    outs, (held, in_sem, out_sem) = refs[stores:-3], refs[-3:]
    count = held.shape[1]
    steps = [(o, at, s, n) for o, pairs in enumerate(plan) for at, (s, n) in enumerate(pairs)]
    for i, (_, _, s, n) in enumerate(steps):
        @pl.loop(0, count)
        def _(j, i=i, s=s, n=n):
            pltpu.make_async_copy(
                refs[s].at[lists_ref[n, j]], held.at[i, j], in_sem.at[i]
            ).start()
    copies = []
    for i, (o, at, _, _) in enumerate(steps):
        pltpu.make_async_copy(held.at[i], held.at[i], in_sem.at[i]).wait()
        copies.append(
            pltpu.make_async_copy(
                held.at[i], outs[o].at[pl.ds(at * count, count)], out_sem.at[i]
            )
        )
        copies[-1].start()
    for copy in copies:
        copy.wait()


def fetch(order, lists, stores, plan):
    count = lists.shape[1]
    shape = stores[0].shape[1:]
    total = sum(map(len, plan))
    outs = order.call(
        functools.partial(fetch_kernel, stores=len(stores), plan=plan),
        lists,
        stores,
        [pl.BlockSpec(memory_space=pl.ANY)] * len(stores),
        out_shape=[jax.ShapeDtypeStruct((len(p) * count,) + shape, BF16) for p in plan],
        grid_spec=dict(
            grid=(1,),
            out_specs=[pl.BlockSpec(memory_space=pl.ANY)] * len(plan),
            scratch_shapes=[
                pltpu.VMEM((total, count) + shape, BF16),
                pltpu.SemaphoreType.DMA((total,)),
                pltpu.SemaphoreType.DMA((total,)),
            ],
        ),
    )
    return [o.reshape(o.shape[0] * shape[0], shape[1]) for o in outs]


def sum_kernel(at_ref, *refs, plan, has_total, has_out, rounded):
    refs = list(refs)
    factors = [([refs.pop(0) for _ in range(n)], refs.pop(0)) for n in plan]
    total = refs.pop(0) if has_total else None
    if has_out:
        refs.pop(0)
    out = refs.pop(0)
    value = total[...] if has_total else None
    for xs, w in factors:
        if len(xs) == 2:
            both = refs.pop(0)

            @pl.when(pl.program_id(0) == 0)
            def _(xs=xs, both=both):
                both[...] = xs[0][...] + xs[1][...]

            x = both
        else:
            x = xs[0]
        product = jnp.dot(x[...], w[...], preferred_element_type=F32)
        value = product if value is None else value + product
    out[...] = value.astype(BF16) if rounded else value


def add_products(order, terms, total=None, take=0, piece=(0, 1), out=None, rounded=False):
    rows = terms[0][0][0].shape[0]
    width = terms[0][1].shape[1]
    tile = min(TILE, width)
    at = jnp.stack([jnp.asarray(t[2], jnp.int32) for t in terms])
    here = piece[0]
    specs, args, scratch = [], [], []
    for n, (xs, w, _) in enumerate(terms):
        depth = xs[0].shape[1]
        for x in xs:
            specs.append(pl.BlockSpec((rows, depth), lambda j, at: (0, 0)))
            args.append(x)
        specs.append(pl.BlockSpec((depth, tile), lambda j, at, n=n: (at[n], j)))
        args.append(w)
        if len(xs) == 2:
            scratch.append(pltpu.VMEM((rows, depth), BF16))
    if total is not None:
        specs.append(pl.BlockSpec((rows, tile), lambda j, at: (take, j)))
        args.append(total)
    aliases = {}
    if out is not None:
        aliases = {len(args) + 1: 0}
        specs.append(pl.BlockSpec(memory_space=pl.ANY))
        args.append(out)
    dtype = BF16 if rounded else F32
    return order.call(
        functools.partial(
            sum_kernel,
            plan=[len(t[0]) for t in terms],
            has_total=total is not None,
            has_out=out is not None,
            rounded=rounded,
        ),
        at,
        args,
        specs,
        out_shape=jax.ShapeDtypeStruct((rows * piece[1], width), dtype),
        grid_spec=dict(
            grid=(width // tile,),
            out_specs=pl.BlockSpec((rows, tile), lambda j, at: (here, j)),
            scratch_shapes=scratch,
        ),
        input_output_aliases=aliases,
    )


def shrink_kernel(at_ref, code_ref, x_ref, *refs, most, rank):
    blocks, out = refs[:-1], refs[-1]
    value = 0.0
    width = most * rank
    place = lax.broadcasted_iota(jnp.int32, (width, 1), 0) // rank
    fold = lax.broadcasted_iota(jnp.int32, (rank, width), 1) % rank == lax.broadcasted_iota(
        jnp.int32, (rank, width), 0
    )
    for n, block in enumerate(blocks):
        product = lax.dot_general(
            block[...], x_ref[...], (((1,), (1,)), ((), ())), preferred_element_type=F32
        )
        value = value + jnp.where(at_ref[n] * most + place == code_ref[...], product, 0.0)
    out[...] = jnp.dot(
        fold.astype(F32), value, precision=lax.Precision.HIGHEST, preferred_element_type=F32
    )


def shrink_parts(order, tokens, blocks, at, code, most, rank, waits=()):
    rows, depth = tokens.shape
    width = most * rank
    full = lambda *_: (0, 0)
    return order.call(
        functools.partial(shrink_kernel, most=most, rank=rank),
        jnp.stack(at),
        [code[None, :], tokens, *blocks],
        [pl.BlockSpec((1, rows), full), pl.BlockSpec((rows, depth), full)]
        + [pl.BlockSpec((width, depth), full)] * len(blocks),
        waits=list(waits),
        out_shape=jax.ShapeDtypeStruct((rank, rows), F32),
        grid_spec=dict(grid=(1,), out_specs=pl.BlockSpec((rank, rows), full)),
    )


def body(
    tokens,
    query_base_weight,
    stored_shrink_factors,
    stored_expand_factors,
    segment_adapter,
    segment_length,
    adapter_storage_slot,
):
    groups = lax.axis_size("dp")
    lanes = lax.axis_size("tensor")
    me = lax.axis_index("dp")
    stored, rank, depth = stored_shrink_factors.shape
    used = segment_adapter.shape[1]
    most = used // 2
    rows = tokens.shape[0]
    count_all = adapter_storage_slot.shape[0]

    flat_ids = segment_adapter.reshape(-1)
    match = flat_ids[:, None] == jnp.arange(count_all, dtype=jnp.int32)[None, :]
    slot = jnp.sum(jnp.where(match, adapter_storage_slot[None, :], 0), axis=1)
    slot = slot.reshape(groups, used)
    home, local = slot // stored, slot % stored

    earlier = jnp.arange(used)[None, :] < jnp.arange(used)[:, None]
    same = home[:, :, None] == home[:, None, :]
    place = jnp.sum(jnp.where(same & earlier[None], 1, 0), axis=2)

    mine = (home == me)[:, :, None] & (place[:, :, None] == jnp.arange(most)[None, None, :])
    lists = jnp.sum(jnp.where(mine, local[:, :, None], 0), axis=1)
    to = me ^ jnp.arange(groups, dtype=jnp.int32)
    lists = jnp.sum(jnp.where((to[:, None] == jnp.arange(groups)[None])[:, :, None], lists[None], 0), axis=1)

    def send(block, k):
        return lax.ppermute(block, "dp", [(i, i ^ k) for i in range(groups)])

    here = (jnp.arange(groups) == me)[:, None]
    code_of = jnp.sum(jnp.where(here, home * most + place, 0), axis=0)
    ends = jnp.cumsum(segment_length[0])
    row_ids = jnp.arange(rows, dtype=jnp.int32)
    starts = ends - segment_length[0]
    member = (starts[None, :] <= row_ids[:, None]) & (row_ids[:, None] < ends[None, :])
    code = jnp.sum(jnp.where(member, code_of[None, :], 0), axis=1)

    half = groups // 2
    order = Order(code)
    stores = [stored_shrink_factors, stored_expand_factors]
    pairs = [(k, k + 1) for k in range(half, groups, 2)]
    far_a = fetch(order, lists, stores, [[(0, k), (0, l)] for k, l in pairs])
    far_a = [send(x, k) for x, (k, _) in zip(far_a, pairs)]
    rest = fetch(
        order,
        lists,
        stores,
        [[(s, k)] for s in range(2) for k in range(half)] + [[(1, k)] for k in range(half, groups)],
    )
    near_a, near_b, far_b = rest[:half], rest[half : 2 * half], rest[2 * half :]
    near_a = near_a[:1] + [send(x, k) for k, x in enumerate(near_a[1:], 1)]
    near_b = near_b[:1] + [send(x, k) for k, x in enumerate(near_b[1:], 1)]

    weight = query_base_weight
    line = lax.axis_index("tensor")

    def shrink_of(blocks, ks):
        return shrink_parts(order, tokens, blocks, [me ^ k for k in ks], code, most, rank)

    part = shrink_of(near_a, range(half))
    near_b = near_b[:1] + [order.hold(x) for x in near_b[1:]]
    if lanes == 4:
        swap = [(0, 1), (1, 0), (2, 3), (3, 2)]
        middle = [(1, 2), (2, 1)]
        outward = [(1, 0), (2, 3)]
        near = order.hold(lax.ppermute(tokens, "tensor", swap))
        cross = order.hold(lax.ppermute(tokens, "tensor", middle))
        far = lax.ppermute(near, "tensor", middle)
        out_near = lax.ppermute(cross, "tensor", outward)
        own = add_products(order, [([tokens], weight, line), ([near], weight, line ^ 1)])

    deep = most * rank
    far_a = [order.hold(x) for x in far_a]
    handed = [
        [send(x[deep + i * deep // 2 : deep + (i + 1) * deep // 2], 1) for i in range(2)]
        for x in far_a
    ]
    part = part + shrink_of(far_a, [k for k, _ in pairs])
    part = part + shrink_of([jnp.concatenate(h) for h in handed], [l for _, l in pairs])
    far_b = [far_b[i] if i % 2 else order.hold(far_b[i]) for i in range(half)]
    far_b = [send(x, k) for k, x in enumerate(far_b, half)]
    if lanes == 4:
        pieces = 2
        step = rows // pieces

        def onward(i):
            return lax.ppermute(far[i * step : (i + 1) * step], "tensor", outward)

        shrink = part + lax.ppermute(part, "tensor", [(i, i ^ 1) for i in range(4)])
        out_near = order.hold(out_near)
        shrink = order.hold(shrink)
        shrink = shrink + lax.ppermute(shrink, "tensor", [(i, i ^ 2) for i in range(4)])
        far = order.hold(far)
        out_far = [onward(i) for i in range(pieces)]
        own = add_products(order, [([far, out_near], weight, line ^ 2)], own)
    else:
        shrink = lax.psum(part, "tensor")
    low = shrink.astype(BF16)
    column = jnp.arange(most * rank, dtype=jnp.int32)
    fold = (column[None, :] % rank == jnp.arange(rank)[:, None]).astype(BF16)
    spread = lax.dot_general(
        low, fold, (((0,), (0,)), ((), ())), preferred_element_type=F32
    ).astype(BF16)

    def chosen(k):
        mine = ((me ^ k) * most + column // rank)[None, :] == code[:, None]
        return jnp.where(mine, spread, jnp.zeros((), BF16))

    near_terms = [([chosen(k)], near_b[k], 0) for k in range(half)]
    far_terms = [([chosen(k)], x, 0) for k, x in enumerate(far_b, half)]

    if lanes != 4:
        whole = lax.all_gather(tokens, "tensor", axis=1, tiled=True)
        base = jnp.dot(whole, weight, preferred_element_type=F32)
        for (x,), w, i in near_terms + far_terms:
            base = base + jnp.dot(x, w[i * deep : (i + 1) * deep], preferred_element_type=F32)
        return base.astype(BF16)

    total = add_products(order, near_terms, own)

    def last_slice(i):
        return [([cross[i * step : (i + 1) * step], out_far[i]], weight, line ^ 3)]

    first = add_products(order, last_slice(0), total, 0)

    def far_part(i):
        return [([x[i * step : (i + 1) * step] for x in xs], w, n) for xs, w, n in far_terms]

    out = add_products(order, far_part(0), first, 0, (0, pieces), None, True)
    second = add_products(order, far_part(1), total, 1)
    return add_products(order, last_slice(1), second, 0, (1, pieces), out, True)


def solution(mesh):
    in_specs = (
        P(("groups", "dp"), "tensor"),
        P(None, "tensor"),
        P("dp", None, "tensor"),
        P("dp", None, "tensor"),
        P("groups", None),
        P(("groups", "dp"), None),
        P("groups"),
    )
    out_specs = P(("groups", "dp"), "tensor")
    return jax.shard_map(body, mesh=mesh, in_specs=in_specs, out_specs=out_specs, check_vma=False)
```

```python
import functools

import jax
import jax.numpy as jnp
from jax import lax
from jax.experimental import pallas as pl
from jax.experimental.pallas import tpu as pltpu
from jax.sharding import PartitionSpec as P

F32 = jnp.float32
BF16 = jnp.bfloat16
ROOM = 48 * 1024 * 1024
TILE = 512


class Order:
    def __init__(self, first):
        self.last = first

    def call(self, kernel, at, args, specs, **rest):
        after = [] if rest.get("input_output_aliases") else [self.last]

        def body(at_ref, *refs):
            kernel(at_ref, *refs[: len(args)], *refs[len(args) + len(after) :])

        outs = pl.pallas_call(
            body,
            grid_spec=pltpu.PrefetchScalarGridSpec(
                num_scalar_prefetch=1,
                in_specs=list(specs) + [pl.BlockSpec(memory_space=pl.ANY)] * len(after),
                **rest.pop("grid_spec"),
            ),
            compiler_params=pltpu.CompilerParams(vmem_limit_bytes=ROOM),
            cost_estimate=pl.CostEstimate(flops=1, bytes_accessed=1, transcendentals=0),
            **rest,
        )(at, *args, *after)
        self.last = outs[0] if isinstance(outs, (list, tuple)) else outs
        return outs


    def hold(self, x):
        self.last = pl.pallas_call(
            lambda *_: None,
            out_shape=jax.ShapeDtypeStruct(x.shape, x.dtype),
            in_specs=[pl.BlockSpec(memory_space=pl.ANY)] * 2,
            out_specs=pl.BlockSpec(memory_space=pl.ANY),
            input_output_aliases={0: 0},
            cost_estimate=pl.CostEstimate(flops=1, bytes_accessed=1, transcendentals=0),
        )(x, self.last)
        return self.last


    def cut(self, x, sizes):
        def kernel(x_ref, _, *outs):
            start = 0
            for size, out in zip(sizes, outs):
                out[...] = x_ref[pl.ds(start, size)]
                start += size

        outs = pl.pallas_call(
            kernel,
            out_shape=[jax.ShapeDtypeStruct((size, x.shape[1]), x.dtype) for size in sizes],
            in_specs=[pl.BlockSpec(memory_space=pltpu.VMEM), pl.BlockSpec(memory_space=pl.ANY)],
            out_specs=[pl.BlockSpec(memory_space=pltpu.VMEM)] * len(sizes),
            compiler_params=pltpu.CompilerParams(vmem_limit_bytes=ROOM),
            cost_estimate=pl.CostEstimate(flops=1, bytes_accessed=1, transcendentals=0),
        )(x, self.last)
        self.last = outs[0]
        return outs


def fetch_kernel(lists_ref, *refs, stores, plan):
    outs, (held, in_sem, out_sem) = refs[stores:-3], refs[-3:]
    count = held.shape[1]
    steps = [(o, at, s, n) for o, pairs in enumerate(plan) for at, (s, n) in enumerate(pairs)]
    for i, (_, _, s, n) in enumerate(steps):
        @pl.loop(0, count)
        def _(j, i=i, s=s, n=n):
            pltpu.make_async_copy(
                refs[s].at[lists_ref[n, j]], held.at[i, j], in_sem.at[i]
            ).start()
    copies = []
    for i, (o, at, _, _) in enumerate(steps):
        pltpu.make_async_copy(held.at[i], held.at[i], in_sem.at[i]).wait()
        copies.append(
            pltpu.make_async_copy(
                held.at[i], outs[o].at[pl.ds(at * count, count)], out_sem.at[i]
            )
        )
        copies[-1].start()
    for copy in copies:
        copy.wait()


def fetch(order, lists, stores, plan):
    count = lists.shape[1]
    shape = stores[0].shape[1:]
    total = sum(map(len, plan))
    outs = order.call(
        functools.partial(fetch_kernel, stores=len(stores), plan=plan),
        lists,
        stores,
        [pl.BlockSpec(memory_space=pl.ANY)] * len(stores),
        out_shape=[jax.ShapeDtypeStruct((len(p) * count,) + shape, BF16) for p in plan],
        grid_spec=dict(
            grid=(1,),
            out_specs=[pl.BlockSpec(memory_space=pl.ANY)] * len(plan),
            scratch_shapes=[
                pltpu.VMEM((total, count) + shape, BF16),
                pltpu.SemaphoreType.DMA((total,)),
                pltpu.SemaphoreType.DMA((total,)),
            ],
        ),
    )
    return [o.reshape(o.shape[0] * shape[0], shape[1]) for o in outs]


def sum_kernel(at_ref, *refs, plan, has_total, has_out, rounded):
    refs = list(refs)
    factors = [([refs.pop(0) for _ in range(n)], refs.pop(0)) for n in plan]
    total = refs.pop(0) if has_total else None
    if has_out:
        refs.pop(0)
    out = refs.pop(0)
    value = total[...] if has_total else None
    for xs, w in factors:
        if len(xs) > 1:
            both = refs.pop(0)

            @pl.when(pl.program_id(0) == 0)
            def _(xs=xs, both=both):
                start = 0
                for x in xs[:-1]:
                    part = pl.ds(start, x.shape[0])
                    both[part] = x[...] + xs[-1][part]
                    start += x.shape[0]

            x = both
        else:
            x = xs[0]
        product = jnp.dot(x[...], w[...], preferred_element_type=F32)
        value = product if value is None else value + product
    out[...] = value.astype(BF16) if rounded else value


def add_products(order, terms, total=None, first=0, rows=None, whole=None, out=None, rounded=False):
    rows = rows or terms[0][0][-1].shape[0]
    width = terms[0][1].shape[1]
    tile = min(TILE, width)
    at = jnp.stack([jnp.asarray(t[2], jnp.int32) for t in terms])
    here = first // rows
    there = here if whole else 0
    specs, args, scratch = [], [], []
    for n, (xs, w, _) in enumerate(terms):
        depth = xs[0].shape[1]
        for x in xs:
            at_row = here if x is xs[-1] and x.shape[0] > rows else 0
            specs.append(
                pl.BlockSpec((min(rows, x.shape[0]), depth), lambda j, at, i=at_row: (i, 0))
            )
            args.append(x)
        specs.append(pl.BlockSpec((depth, tile), lambda j, at, n=n: (at[n], j)))
        args.append(w)
        if len(xs) > 1:
            scratch.append(pltpu.VMEM((rows, depth), BF16))
    if total is not None:
        specs.append(pl.BlockSpec((rows, tile), lambda j, at: (here, j)))
        args.append(total)
    aliases = {}
    if out is not None:
        aliases = {len(args) + 1: 0}
        specs.append(pl.BlockSpec(memory_space=pl.ANY))
        args.append(out)
    dtype = BF16 if rounded else F32
    return order.call(
        functools.partial(
            sum_kernel,
            plan=[len(t[0]) for t in terms],
            has_total=total is not None,
            has_out=out is not None,
            rounded=rounded,
        ),
        at,
        args,
        specs,
        out_shape=jax.ShapeDtypeStruct((whole or rows, width), dtype),
        grid_spec=dict(
            grid=(width // tile,),
            out_specs=pl.BlockSpec((rows, tile), lambda j, at: (there, j)),
            scratch_shapes=scratch,
        ),
        input_output_aliases=aliases,
    )


def expand_kernel(at_ref, low, codes, *refs, most, rank):
    blocks, (total, out, picks) = refs[:-3], refs[-3:]
    width = most * rank

    @pl.when(pl.program_id(0) == 0)
    def _():
        column = lax.broadcasted_iota(jnp.int32, (rank, width), 1)
        fold = column % rank == lax.broadcasted_iota(jnp.int32, (rank, width), 0)
        spread = lax.dot_general(
            low[...], fold.astype(BF16), (((0,), (0,)), ((), ())), preferred_element_type=F32
        )
        place = lax.broadcasted_iota(jnp.int32, (1, width), 1) // rank
        for n in range(len(blocks)):
            mine = codes[...] == at_ref[len(blocks) + n] * most + place
            picks[n] = jnp.where(mine, spread, 0.0).astype(BF16)

    value = total[...]
    for n, block in enumerate(blocks):
        value = value + jnp.dot(picks[n], block[...], preferred_element_type=F32)
    out[...] = value


def add_expanded(order, low, codes, factors, homes, total, most):
    rank, rows = low.shape
    width = total.shape[1]
    tile = min(TILE, width)
    at = jnp.stack([jnp.asarray(x, jnp.int32) for x in [i for _, i in factors] + homes])
    full = lambda j, at: (0, 0)
    return order.call(
        functools.partial(expand_kernel, most=most, rank=rank),
        at,
        [low, codes, *[w for w, _ in factors], total],
        [pl.BlockSpec((rank, rows), full), pl.BlockSpec((rows, 1), full)]
        + [
            pl.BlockSpec((most * rank, tile), lambda j, at, n=n: (at[n], j))
            for n in range(len(factors))
        ]
        + [pl.BlockSpec((rows, tile), lambda j, at: (0, j))],
        out_shape=jax.ShapeDtypeStruct((rows, width), F32),
        grid_spec=dict(
            grid=(width // tile,),
            out_specs=pl.BlockSpec((rows, tile), lambda j, at: (0, j)),
            scratch_shapes=[pltpu.VMEM((len(factors), rows, most * rank), BF16)],
        ),
    )


def shrink_kernel(at_ref, code, x, store, mates, out, held, sem, *, k, most, rank):
    for i in range(2):
        @pl.loop(0, most // 2)
        def _(j, i=i):
            j = j + i * (most // 2)
            pltpu.make_async_copy(
                store.at[at_ref[k, j]], held.at[pl.ds(j * rank, rank)], sem
            ).start()
    width = most * rank
    place = lax.broadcasted_iota(jnp.int32, (width, 1), 0) // rank
    fold = lax.broadcasted_iota(jnp.int32, (rank, width), 1) % rank == lax.broadcasted_iota(
        jnp.int32, (rank, width), 0
    )

    last = at_ref.shape[0] - 1

    def picked(block, which):
        product = lax.dot_general(
            block, x[...], (((1,), (1,)), ((), ())), preferred_element_type=F32
        )
        return jnp.where(at_ref[last, which] * most + place == code[...], product, 0.0)

    value = picked(mates[...], 1)
    pltpu.make_async_copy(held, held, sem).wait()
    out[...] = jnp.dot(
        fold.astype(F32),
        value + picked(held[...], 0),
        precision=lax.Precision.HIGHEST,
        preferred_element_type=F32,
    )


def shrink_part(order, lists, k, code, x, store, mates):
    rows, depth = code.shape[1], x.shape[1]
    most, rank = lists.shape[1], store.shape[1]
    full = lambda i, at: (0, 0)
    return order.call(
        functools.partial(shrink_kernel, k=k, most=most, rank=rank),
        lists,
        [code, x, store, mates],
        [
            pl.BlockSpec((1, rows), full),
            pl.BlockSpec((rows, depth), full),
            pl.BlockSpec(memory_space=pl.ANY),
            pl.BlockSpec((most * rank, depth), full),
        ],
        out_shape=jax.ShapeDtypeStruct((rank, rows), F32),
        grid_spec=dict(
            grid=(1,),
            out_specs=pl.BlockSpec((rank, rows), full),
            scratch_shapes=[
                pltpu.VMEM((most * rank, depth), BF16),
                pltpu.SemaphoreType.DMA(()),
            ],
        ),
    )


def body(
    tokens,
    query_base_weight,
    stored_shrink_factors,
    stored_expand_factors,
    segment_adapter,
    segment_length,
    adapter_storage_slot,
):
    groups = lax.axis_size("dp")
    lanes = lax.axis_size("tensor")
    me = lax.axis_index("dp")
    stored, rank, depth = stored_shrink_factors.shape
    used = segment_adapter.shape[1]
    most = used // 2
    rows = tokens.shape[0]
    count_all = adapter_storage_slot.shape[0]

    flat_ids = segment_adapter.reshape(-1)
    match = flat_ids[:, None] == jnp.arange(count_all, dtype=jnp.int32)[None, :]
    slot = jnp.sum(jnp.where(match, adapter_storage_slot[None, :], 0), axis=1)
    slot = slot.reshape(groups, used)
    home, local = slot // stored, slot % stored

    earlier = jnp.arange(used)[None, :] < jnp.arange(used)[:, None]
    same = home[:, :, None] == home[:, None, :]
    place = jnp.sum(jnp.where(same & earlier[None], 1, 0), axis=2)

    mine = (home == me)[:, :, None] & (place[:, :, None] == jnp.arange(most)[None, None, :])
    lists = jnp.sum(jnp.where(mine, local[:, :, None], 0), axis=1)
    to = me ^ jnp.arange(groups, dtype=jnp.int32)
    lists = jnp.sum(jnp.where((to[:, None] == jnp.arange(groups)[None])[:, :, None], lists[None], 0), axis=1)

    def send(block, k):
        return lax.ppermute(block, "dp", [(i, i ^ k) for i in range(groups)])

    here = (jnp.arange(groups) == me)[:, None]
    code_of = jnp.sum(jnp.where(here, home * most + place, 0), axis=0)
    ends = jnp.cumsum(segment_length[0])
    row_ids = jnp.arange(rows, dtype=jnp.int32)
    member = ((ends - segment_length[0])[None, :] <= row_ids[:, None]) & (
        row_ids[:, None] < ends[None, :]
    )
    code = jnp.sum(jnp.where(member, code_of[None, :], 0), axis=1)
    note = jnp.pad(code, (0, 16 * depth - rows)).reshape(16, depth).astype(BF16)
    noted = jnp.concatenate([tokens, note], axis=0)

    homes = jnp.where(jnp.arange(most) == 0, me, me ^ 1)[None]
    lists = jnp.concatenate([lists, homes])
    order = Order(lists)
    weight = query_base_weight
    line = lax.axis_index("tensor")
    shrinks, expands = stored_shrink_factors, stored_expand_factors
    across = send(noted, 2)
    plan = [[p] for p in [(0, 1), (0, 3), (1, 1), (1, 0), (1, 2), (1, 3)]]
    blocks = fetch(order, lists, [shrinks, expands], plan)
    mates = [send(x, 1) for x in blocks[:3]]
    far_b = [None, send(blocks[5], 3)]

    def shrink_of(k, code, x, mates):
        return shrink_part(order, lists, k, code[None], x, shrinks, mates)

    if lanes == 4:
        swap = [(0, 1), (1, 0), (2, 3), (3, 2)]
        middle = [(1, 2), (2, 1)]
        inward = [(0, 1), (3, 2)]
        outward = [(1, 0), (2, 3)]
        step = rows // 4
        near = lax.ppermute(tokens, "tensor", swap)
        cross = lax.ppermute(tokens, "tensor", middle)
        own = add_products(order, [([tokens], weight, line)])
        cross = order.hold(cross)
        out_near = lax.ppermute(cross, "tensor", outward)
        cuts = order.cut(near, [2 * step] * 2)
        far = [lax.ppermute(x, "tensor", middle) for x in cuts]
        across = order.hold(across)
        own = add_products(order, [([near], weight, line ^ 1)], own)
    part = shrink_of(0, code, tokens, mates[0])
    code_across = across[rows:].reshape(-1)[:rows].astype(F32).astype(jnp.int32)
    part = part + send(shrink_of(2, code_across, across, mates[1]), 2)
    if lanes == 4:
        far[0] = order.hold(far[0])
        out_far = [lax.ppermute(far[0], "tensor", outward)]
        far_b[1] = order.hold(far_b[1])
        part = order.hold(part)
        far_b[0] = send(order.hold(blocks[4]), 2)
        out_near = order.hold(out_near)
        part = order.hold(part + lax.ppermute(part, "tensor", inward))
        part = part + lax.ppermute(part, "tensor", middle)
        own = add_products(order, [([*far, out_near], weight, line ^ 2)], own)
        low = order.hold(part.astype(BF16))
        told = lax.ppermute(low, "tensor", outward)
        pieces = order.cut(far[1], [step] * 2)
        out_far.append(lax.ppermute(pieces[0], "tensor", outward))
        told = order.hold(told)
        out_far.append(lax.ppermute(order.hold(pieces[1]), "tensor", outward))
        low = jnp.where((line == 1) | (line == 2), low, told)
    else:
        far_b[0] = send(blocks[4], 2)
        low = lax.psum(part, "tensor").astype(BF16)
    factors = [(x, 0) for x in (blocks[3], mates[2], *far_b)]
    if lanes != 4:
        whole = lax.all_gather(tokens, "tensor", axis=1, tiled=True)
        own = jnp.dot(whole, weight, preferred_element_type=F32)
    total = add_expanded(order, low, code[:, None], factors, [me ^ k for k in range(groups)], own, most)
    if lanes != 4:
        return total.astype(BF16)
    out = None
    first = 0
    for x in out_far:
        last = [([x, cross], weight, line ^ 3)]
        out = add_products(order, last, total, first, x.shape[0], rows, out, True)
        first += x.shape[0]
    return out


def solution(mesh):
    in_specs = (
        P(("groups", "dp"), "tensor"),
        P(None, "tensor"),
        P("dp", None, "tensor"),
        P("dp", None, "tensor"),
        P("groups", None),
        P(("groups", "dp"), None),
        P("groups"),
    )
    out_specs = P(("groups", "dp"), "tensor")
    return jax.shard_map(body, mesh=mesh, in_specs=in_specs, out_specs=out_specs, check_vma=False)
```

```python
import functools

import jax
import jax.numpy as jnp
from jax import lax
from jax.experimental import pallas as pl
from jax.experimental.pallas import tpu as pltpu
from jax.sharding import PartitionSpec as P

F32 = jnp.float32
BF16 = jnp.bfloat16
ROOM = 36 * 1024 * 1024
TILE = 512


class Order:
    def __init__(self, first):
        self.last = first

    def call(self, kernel, at, args, specs, room=ROOM, **rest):
        after = [] if rest.get("input_output_aliases") else [self.last]

        def body(at_ref, *refs):
            kernel(at_ref, *refs[: len(args)], *refs[len(args) + len(after) :])

        outs = pl.pallas_call(
            body,
            grid_spec=pltpu.PrefetchScalarGridSpec(
                num_scalar_prefetch=1,
                in_specs=list(specs) + [pl.BlockSpec(memory_space=pl.ANY)] * len(after),
                **rest.pop("grid_spec"),
            ),
            compiler_params=pltpu.CompilerParams(vmem_limit_bytes=room),
            cost_estimate=pl.CostEstimate(flops=1, bytes_accessed=1, transcendentals=0),
            **rest,
        )(at, *args, *after)
        self.last = outs[0] if isinstance(outs, (list, tuple)) else outs
        return outs


    def hold(self, x):
        self.last = pl.pallas_call(
            lambda *_: None,
            out_shape=jax.ShapeDtypeStruct(x.shape, x.dtype),
            in_specs=[pl.BlockSpec(memory_space=pl.ANY)] * 2,
            out_specs=pl.BlockSpec(memory_space=pl.ANY),
            input_output_aliases={0: 0},
            cost_estimate=pl.CostEstimate(flops=1, bytes_accessed=1, transcendentals=0),
        )(x, self.last)
        return self.last


    def cut(self, x, sizes):
        def kernel(x_ref, _, *outs):
            start = 0
            for size, out in zip(sizes, outs):
                out[...] = x_ref[pl.ds(start, size)]
                start += size

        outs = pl.pallas_call(
            kernel,
            out_shape=[jax.ShapeDtypeStruct((size, x.shape[1]), x.dtype) for size in sizes],
            in_specs=[pl.BlockSpec(memory_space=pltpu.VMEM), pl.BlockSpec(memory_space=pl.ANY)],
            out_specs=[pl.BlockSpec(memory_space=pltpu.VMEM)] * len(sizes),
            compiler_params=pltpu.CompilerParams(vmem_limit_bytes=ROOM),
            cost_estimate=pl.CostEstimate(flops=1, bytes_accessed=1, transcendentals=0),
        )(x, self.last)
        self.last = outs[0]
        return outs


def fetch_kernel(lists_ref, *refs, stores, plan):
    outs, (held, in_sem, out_sem) = refs[stores:-3], refs[-3:]
    count = held.shape[1]
    steps = [(o, at, s, n) for o, pairs in enumerate(plan) for at, (s, n) in enumerate(pairs)]
    for i, (_, _, s, n) in enumerate(steps):
        @pl.loop(0, count)
        def _(j, i=i, s=s, n=n):
            pltpu.make_async_copy(
                refs[s].at[lists_ref[n, j]], held.at[i, j], in_sem.at[i]
            ).start()
    copies = []
    for i, (o, at, _, _) in enumerate(steps):
        pltpu.make_async_copy(held.at[i], held.at[i], in_sem.at[i]).wait()
        copies.append(
            pltpu.make_async_copy(
                held.at[i], outs[o].at[pl.ds(at * count, count)], out_sem.at[i]
            )
        )
        copies[-1].start()
    for copy in copies:
        copy.wait()


def fetch(order, lists, stores, plan):
    count = lists.shape[1]
    shape = stores[0].shape[1:]
    total = sum(map(len, plan))
    outs = order.call(
        functools.partial(fetch_kernel, stores=len(stores), plan=plan),
        lists,
        stores,
        [pl.BlockSpec(memory_space=pl.ANY)] * len(stores),
        out_shape=[jax.ShapeDtypeStruct((len(p) * count,) + shape, BF16) for p in plan],
        grid_spec=dict(
            grid=(1,),
            out_specs=[pl.BlockSpec(memory_space=pl.ANY)] * len(plan),
            scratch_shapes=[
                pltpu.VMEM((total, count) + shape, BF16),
                pltpu.SemaphoreType.DMA((total,)),
                pltpu.SemaphoreType.DMA((total,)),
            ],
        ),
    )
    return [o.reshape(o.shape[0] * shape[0], shape[1]) for o in outs]


def sum_kernel(at_ref, *refs, plan, has_total, has_out, rounded):
    refs = list(refs)
    factors = [([refs.pop(0) for _ in range(n)], refs.pop(0)) for n in plan]
    total = refs.pop(0) if has_total else None
    if has_out:
        refs.pop(0)
    out = refs.pop(0)
    value = total[...] if has_total else None
    for xs, w in factors:
        if len(xs) > 1:
            both = refs.pop(0)

            @pl.when(pl.program_id(0) == 0)
            def _(xs=xs, both=both):
                start = 0
                for x in xs[:-1]:
                    part = pl.ds(start, x.shape[0])
                    both[part] = x[...] + xs[-1][part]
                    start += x.shape[0]

            x = both
        else:
            x = xs[0]
        product = jnp.dot(x[...], w[...], preferred_element_type=F32)
        value = product if value is None else value + product
    out[...] = value.astype(BF16) if rounded else value


def add_products(order, terms, total=None, first=0, rows=None, whole=None, out=None, rounded=False, room=ROOM):
    rows = rows or terms[0][0][-1].shape[0]
    width = terms[0][1].shape[1]
    tile = min(2 * TILE if rounded else TILE, width)
    at = jnp.stack([jnp.asarray(t[2], jnp.int32) for t in terms])
    here = first // rows
    there = here if whole else 0
    specs, args, scratch = [], [], []
    for n, (xs, w, _) in enumerate(terms):
        depth = xs[0].shape[1]
        for x in xs:
            at_row = here if x is xs[-1] and x.shape[0] > rows else 0
            specs.append(
                pl.BlockSpec((min(rows, x.shape[0]), depth), lambda j, at, i=at_row: (i, 0))
            )
            args.append(x)
        specs.append(pl.BlockSpec((depth, tile), lambda j, at, n=n: (at[n], j)))
        args.append(w)
        if len(xs) > 1:
            scratch.append(pltpu.VMEM((rows, depth), BF16))
    if total is not None:
        specs.append(pl.BlockSpec((rows, tile), lambda j, at: (here, j)))
        args.append(total)
    aliases = {}
    if out is not None:
        aliases = {len(args) + 1: 0}
        specs.append(pl.BlockSpec(memory_space=pl.ANY))
        args.append(out)
    dtype = BF16 if rounded else F32
    return order.call(
        functools.partial(
            sum_kernel,
            plan=[len(t[0]) for t in terms],
            has_total=total is not None,
            has_out=out is not None,
            rounded=rounded,
        ),
        at,
        args,
        specs,
        room,
        out_shape=jax.ShapeDtypeStruct((whole or rows, width), dtype),
        grid_spec=dict(
            grid=(width // tile,),
            out_specs=pl.BlockSpec((rows, tile), lambda j, at: (there, j)),
            scratch_shapes=scratch,
        ),
        input_output_aliases=aliases,
    )


def expand_kernel(at_ref, low, codes, *refs, most, rank):
    blocks, (total, out, picks) = refs[:-3], refs[-3:]
    width = most * rank

    @pl.when(pl.program_id(0) == 0)
    def _():
        column = lax.broadcasted_iota(jnp.int32, (rank, width), 1)
        fold = column % rank == lax.broadcasted_iota(jnp.int32, (rank, width), 0)
        spread = lax.dot_general(
            low[...], fold.astype(BF16), (((0,), (0,)), ((), ())), preferred_element_type=F32
        )
        place = lax.broadcasted_iota(jnp.int32, (1, width), 1) // rank
        for n in range(len(blocks)):
            mine = codes[...] == at_ref[len(blocks) + n] * most + place
            picks[n] = jnp.where(mine, spread, 0.0).astype(BF16)

    value = total[...]
    for n, block in enumerate(blocks):
        value = value + jnp.dot(picks[n], block[...], preferred_element_type=F32)
    out[...] = value


def add_expanded(order, low, codes, factors, homes, total, most):
    rank, rows = low.shape
    width = total.shape[1]
    tile = min(TILE, width)
    at = jnp.stack([jnp.asarray(x, jnp.int32) for x in [i for _, i in factors] + homes])
    full = lambda j, at: (0, 0)
    return order.call(
        functools.partial(expand_kernel, most=most, rank=rank),
        at,
        [low, codes, *[w for w, _ in factors], total],
        [pl.BlockSpec((rank, rows), full), pl.BlockSpec((rows, 1), full)]
        + [
            pl.BlockSpec((most * rank, tile), lambda j, at, n=n: (at[n], j))
            for n in range(len(factors))
        ]
        + [pl.BlockSpec((rows, tile), lambda j, at: (0, j))],
        out_shape=jax.ShapeDtypeStruct((rows, width), F32),
        grid_spec=dict(
            grid=(width // tile,),
            out_specs=pl.BlockSpec((rows, tile), lambda j, at: (0, j)),
            scratch_shapes=[pltpu.VMEM((len(factors), rows, most * rank), BF16)],
        ),
    )


def block_of(order, matrix, at, depth):
    width = matrix.shape[1]
    tile = depth // 4

    def kernel(at_ref, x, out):
        out[...] = x[...]

    return order.call(
        kernel,
        jnp.asarray(at, jnp.int32)[None],
        [matrix],
        [pl.BlockSpec((tile, width), lambda i, at: (4 * at[0] + i, 0))],
        out_shape=jax.ShapeDtypeStruct((depth, width), matrix.dtype),
        grid_spec=dict(grid=(4,), out_specs=pl.BlockSpec((tile, width), lambda i, at: (i, 0))),
    )


def shrink_kernel(at_ref, code, x, store, mates, out, held, sem, *, k, most, rank):
    for i in range(2):
        @pl.loop(0, most // 2)
        def _(j, i=i):
            j = j + i * (most // 2)
            pltpu.make_async_copy(
                store.at[at_ref[k, j]], held.at[pl.ds(j * rank, rank)], sem
            ).start()
    width = most * rank
    place = lax.broadcasted_iota(jnp.int32, (width, 1), 0) // rank
    fold = lax.broadcasted_iota(jnp.int32, (rank, width), 1) % rank == lax.broadcasted_iota(
        jnp.int32, (rank, width), 0
    )

    last = at_ref.shape[0] - 1

    def picked(block, which):
        product = lax.dot_general(
            block, x[...], (((1,), (1,)), ((), ())), preferred_element_type=F32
        )
        return jnp.where(at_ref[last, which] * most + place == code[...], product, 0.0)

    value = picked(mates[...], 1)
    pltpu.make_async_copy(held, held, sem).wait()
    out[...] = jnp.dot(
        fold.astype(F32),
        value + picked(held[...], 0),
        precision=lax.Precision.HIGHEST,
        preferred_element_type=F32,
    )


def shrink_part(order, lists, k, code, x, store, mates):
    rows, depth = code.shape[1], x.shape[1]
    most, rank = lists.shape[1], store.shape[1]
    full = lambda i, at: (0, 0)
    return order.call(
        functools.partial(shrink_kernel, k=k, most=most, rank=rank),
        lists,
        [code, x, store, mates],
        [
            pl.BlockSpec((1, rows), full),
            pl.BlockSpec((rows, depth), full),
            pl.BlockSpec(memory_space=pl.ANY),
            pl.BlockSpec((most * rank, depth), full),
        ],
        out_shape=jax.ShapeDtypeStruct((rank, rows), F32),
        grid_spec=dict(
            grid=(1,),
            out_specs=pl.BlockSpec((rank, rows), full),
            scratch_shapes=[
                pltpu.VMEM((most * rank, depth), BF16),
                pltpu.SemaphoreType.DMA(()),
            ],
        ),
    )


def body(
    tokens,
    query_base_weight,
    stored_shrink_factors,
    stored_expand_factors,
    segment_adapter,
    segment_length,
    adapter_storage_slot,
):
    groups = lax.axis_size("dp")
    lanes = lax.axis_size("tensor")
    me = lax.axis_index("dp")
    stored, rank, depth = stored_shrink_factors.shape
    used = segment_adapter.shape[1]
    most = used // 2
    rows = tokens.shape[0]
    count_all = adapter_storage_slot.shape[0]

    flat_ids = segment_adapter.reshape(-1)
    match = flat_ids[:, None] == jnp.arange(count_all, dtype=jnp.int32)[None, :]
    slot = jnp.sum(jnp.where(match, adapter_storage_slot[None, :], 0), axis=1)
    slot = slot.reshape(groups, used)
    home, local = slot // stored, slot % stored

    earlier = jnp.arange(used)[None, :] < jnp.arange(used)[:, None]
    same = home[:, :, None] == home[:, None, :]
    place = jnp.sum(jnp.where(same & earlier[None], 1, 0), axis=2)

    mine = (home == me)[:, :, None] & (place[:, :, None] == jnp.arange(most)[None, None, :])
    lists = jnp.sum(jnp.where(mine, local[:, :, None], 0), axis=1)
    to = me ^ jnp.arange(groups, dtype=jnp.int32)
    lists = jnp.sum(jnp.where((to[:, None] == jnp.arange(groups)[None])[:, :, None], lists[None], 0), axis=1)

    def send(block, k):
        return lax.ppermute(block, "dp", [(i, i ^ k) for i in range(groups)])

    here = (jnp.arange(groups) == me)[:, None]
    code_of = jnp.sum(jnp.where(here, home * most + place, 0), axis=0)
    ends = jnp.cumsum(segment_length[0])
    row_ids = jnp.arange(rows, dtype=jnp.int32)
    member = ((ends - segment_length[0])[None, :] <= row_ids[:, None]) & (
        row_ids[:, None] < ends[None, :]
    )
    code = jnp.sum(jnp.where(member, code_of[None, :], 0), axis=1)
    note = jnp.pad(code, (0, 16 * depth - rows)).reshape(16, depth).astype(BF16)
    noted = jnp.concatenate([tokens, note], axis=0)

    homes = jnp.where(jnp.arange(most) == 0, me, me ^ 1)[None]
    lists = jnp.concatenate([lists, homes])
    order = Order(lists)
    weight = query_base_weight
    line = lax.axis_index("tensor")
    shrinks, expands = stored_shrink_factors, stored_expand_factors
    across = send(noted, 2)
    plan = [[p] for p in [(0, 1), (0, 3), (1, 1), (1, 0), (1, 2), (1, 3)]]
    blocks = fetch(order, lists, [shrinks, expands], plan)
    mates = [send(x, 1) for x in blocks[:3]]
    far_b = [None, send(blocks[5], 3)]

    def shrink_of(k, code, x, mates):
        return shrink_part(order, lists, k, code[None], x, shrinks, mates)

    if lanes == 4:
        swap = [(0, 1), (1, 0), (2, 3), (3, 2)]
        middle = [(1, 2), (2, 1)]
        inward = [(0, 1), (3, 2)]
        outward = [(1, 0), (2, 3)]
        step = rows // 4
        near = lax.ppermute(tokens, "tensor", swap)
        cross = lax.ppermute(tokens, "tensor", middle)
        own = add_products(order, [([tokens], weight, line)], room=62 * 1024 * 1024)
        cross = order.hold(cross)
        out_near = lax.ppermute(cross, "tensor", outward)
        cuts = order.cut(near, [2 * step] * 2)
        far = [lax.ppermute(x, "tensor", middle) for x in cuts]
        across = order.hold(across)
        own = add_products(order, [([near], weight, line ^ 1)], own)
    part = shrink_of(0, code, tokens, mates[0])
    code_across = across[rows:].reshape(-1)[:rows].astype(F32).astype(jnp.int32)
    part = part + send(shrink_of(2, code_across, across, mates[1]), 2)
    if lanes == 4:
        far[0] = order.hold(far[0])
        out_far = [lax.ppermute(far[0], "tensor", outward)]
        far_b[1] = order.hold(far_b[1])
        part = order.hold(part)
        far_b[0] = send(order.hold(blocks[4]), 2)
        out_near = order.hold(out_near)
        part = order.hold(part + lax.ppermute(part, "tensor", inward))
        part = part + lax.ppermute(part, "tensor", middle)
        own = add_products(order, [([*far, out_near], weight, line ^ 2)], own)
        low = order.hold(part.astype(BF16))
        told = lax.ppermute(low, "tensor", outward)
        pieces = order.cut(far[1], [step] * 2)
        out_far.append(lax.ppermute(pieces[0], "tensor", outward))
        last = block_of(order, weight, line ^ 3, depth)
        told = order.hold(told)
        out_far.append(lax.ppermute(order.hold(pieces[1]), "tensor", outward))
        low = jnp.where((line == 1) | (line == 2), low, told)
    else:
        far_b[0] = send(blocks[4], 2)
        low = lax.psum(part, "tensor").astype(BF16)
    factors = [(x, 0) for x in (blocks[3], mates[2], *far_b)]
    if lanes != 4:
        whole = lax.all_gather(tokens, "tensor", axis=1, tiled=True)
        own = jnp.dot(whole, weight, preferred_element_type=F32)
    total = add_expanded(order, low, code[:, None], factors, [me ^ k for k in range(groups)], own, most)
    if lanes != 4:
        return total.astype(BF16)
    out = None
    first = 0
    for x in out_far:
        out = add_products(order, [([x, cross], last, 0)], total, first, x.shape[0], rows, out, True)
        first += x.shape[0]
    return out


def solution(mesh):
    in_specs = (
        P(("groups", "dp"), "tensor"),
        P(None, "tensor"),
        P("dp", None, "tensor"),
        P("dp", None, "tensor"),
        P("groups", None),
        P(("groups", "dp"), None),
        P("groups"),
    )
    out_specs = P(("groups", "dp"), "tensor")
    return jax.shard_map(body, mesh=mesh, in_specs=in_specs, out_specs=out_specs, check_vma=False)
```

```python
import functools

import jax
import jax.numpy as jnp
from jax import lax
from jax.experimental import pallas as pl
from jax.experimental.pallas import tpu as pltpu
from jax.sharding import PartitionSpec as P

F32 = jnp.float32
BF16 = jnp.bfloat16
ROOM = 36 * 1024 * 1024
TILE = 512


class Order:
    def __init__(self, first):
        self.last = first

    def call(self, kernel, at, args, specs, room=ROOM, **rest):
        after = [] if rest.get("input_output_aliases") else [self.last]

        def body(at_ref, *refs):
            kernel(at_ref, *refs[: len(args)], *refs[len(args) + len(after) :])

        outs = pl.pallas_call(
            body,
            grid_spec=pltpu.PrefetchScalarGridSpec(
                num_scalar_prefetch=1,
                in_specs=list(specs) + [pl.BlockSpec(memory_space=pl.ANY)] * len(after),
                **rest.pop("grid_spec"),
            ),
            compiler_params=pltpu.CompilerParams(vmem_limit_bytes=room),
            cost_estimate=pl.CostEstimate(flops=1, bytes_accessed=1, transcendentals=0),
            **rest,
        )(at, *args, *after)
        self.last = outs[0] if isinstance(outs, (list, tuple)) else outs
        return outs


    def hold(self, x):
        self.last = pl.pallas_call(
            lambda *_: None,
            out_shape=jax.ShapeDtypeStruct(x.shape, x.dtype),
            in_specs=[pl.BlockSpec(memory_space=pl.ANY)] * 2,
            out_specs=pl.BlockSpec(memory_space=pl.ANY),
            input_output_aliases={0: 0},
            cost_estimate=pl.CostEstimate(flops=1, bytes_accessed=1, transcendentals=0),
        )(x, self.last)
        return self.last


    def cut(self, x, sizes):
        def kernel(x_ref, _, *outs):
            start = 0
            for size, out in zip(sizes, outs):
                out[...] = x_ref[pl.ds(start, size)]
                start += size

        outs = pl.pallas_call(
            kernel,
            out_shape=[jax.ShapeDtypeStruct((size, x.shape[1]), x.dtype) for size in sizes],
            in_specs=[pl.BlockSpec(memory_space=pltpu.VMEM), pl.BlockSpec(memory_space=pl.ANY)],
            out_specs=[pl.BlockSpec(memory_space=pltpu.VMEM)] * len(sizes),
            compiler_params=pltpu.CompilerParams(vmem_limit_bytes=ROOM),
            cost_estimate=pl.CostEstimate(flops=1, bytes_accessed=1, transcendentals=0),
        )(x, self.last)
        self.last = outs[0]
        return outs


def fetch_kernel(lists_ref, *refs, stores, plan):
    outs, (held, in_sem, out_sem) = refs[stores:-3], refs[-3:]
    count = held.shape[1]
    steps = [(o, at, s, n) for o, pairs in enumerate(plan) for at, (s, n) in enumerate(pairs)]
    for i, (_, _, s, n) in enumerate(steps):
        @pl.loop(0, count)
        def _(j, i=i, s=s, n=n):
            pltpu.make_async_copy(
                refs[s].at[lists_ref[n, j]], held.at[i, j], in_sem.at[i]
            ).start()
    copies = []
    for i, (o, at, _, _) in enumerate(steps):
        pltpu.make_async_copy(held.at[i], held.at[i], in_sem.at[i]).wait()
        copies.append(
            pltpu.make_async_copy(
                held.at[i], outs[o].at[pl.ds(at * count, count)], out_sem.at[i]
            )
        )
        copies[-1].start()
    for copy in copies:
        copy.wait()


def fetch(order, lists, stores, plan):
    count = lists.shape[1]
    shape = stores[0].shape[1:]
    total = sum(map(len, plan))
    outs = order.call(
        functools.partial(fetch_kernel, stores=len(stores), plan=plan),
        lists,
        stores,
        [pl.BlockSpec(memory_space=pl.ANY)] * len(stores),
        out_shape=[jax.ShapeDtypeStruct((len(p) * count,) + shape, BF16) for p in plan],
        grid_spec=dict(
            grid=(1,),
            out_specs=[pl.BlockSpec(memory_space=pl.ANY)] * len(plan),
            scratch_shapes=[
                pltpu.VMEM((total, count) + shape, BF16),
                pltpu.SemaphoreType.DMA((total,)),
                pltpu.SemaphoreType.DMA((total,)),
            ],
        ),
    )
    return [o.reshape(o.shape[0] * shape[0], shape[1]) for o in outs]


def sum_kernel(at_ref, *refs, plan, has_total, has_out, rounded):
    refs = list(refs)
    factors = [([refs.pop(0) for _ in range(n)], refs.pop(0)) for n in plan]
    total = refs.pop(0) if has_total else None
    if has_out:
        refs.pop(0)
    out = refs.pop(0)
    value = total[...] if has_total else None
    for xs, w in factors:
        if len(xs) > 1:
            both = refs.pop(0)

            @pl.when(pl.program_id(0) == 0)
            def _(xs=xs, both=both):
                start = 0
                for x in xs[:-1]:
                    part = pl.ds(start, x.shape[0])
                    both[part] = x[...] + xs[-1][part]
                    start += x.shape[0]

            x = both
        else:
            x = xs[0]
        product = jnp.dot(x[...], w[...], preferred_element_type=F32)
        value = product if value is None else value + product
    out[...] = value.astype(BF16) if rounded else value


def add_products(order, terms, total=None, first=0, rows=None, whole=None, out=None, rounded=False, room=ROOM):
    rows = rows or terms[0][0][-1].shape[0]
    width = terms[0][1].shape[1]
    tile = min(4 * TILE if rounded and rows <= 192 else 2 * TILE if rounded else TILE, width)
    at = jnp.stack([jnp.asarray(t[2], jnp.int32) for t in terms])
    here = first // rows
    there = here if whole else 0
    specs, args, scratch = [], [], []
    for n, (xs, w, _) in enumerate(terms):
        depth = xs[0].shape[1]
        for x in xs:
            at_row = here if x is xs[-1] and x.shape[0] > rows else 0
            specs.append(
                pl.BlockSpec((min(rows, x.shape[0]), depth), lambda j, at, i=at_row: (i, 0))
            )
            args.append(x)
        specs.append(pl.BlockSpec((depth, tile), lambda j, at, n=n: (at[n], j)))
        args.append(w)
        if len(xs) > 1:
            scratch.append(pltpu.VMEM((rows, depth), BF16))
    if total is not None:
        specs.append(pl.BlockSpec((rows, tile), lambda j, at: (here, j)))
        args.append(total)
    aliases = {}
    if out is not None:
        aliases = {len(args) + 1: 0}
        specs.append(pl.BlockSpec(memory_space=pl.ANY))
        args.append(out)
    dtype = BF16 if rounded else F32
    return order.call(
        functools.partial(
            sum_kernel,
            plan=[len(t[0]) for t in terms],
            has_total=total is not None,
            has_out=out is not None,
            rounded=rounded,
        ),
        at,
        args,
        specs,
        room,
        out_shape=jax.ShapeDtypeStruct((whole or rows, width), dtype),
        grid_spec=dict(
            grid=(width // tile,),
            out_specs=pl.BlockSpec((rows, tile), lambda j, at: (there, j)),
            scratch_shapes=scratch,
        ),
        input_output_aliases=aliases,
    )


def expand_kernel(at_ref, low, codes, *refs, most, rank):
    blocks, (total, out, picks) = refs[:-3], refs[-3:]
    width = most * rank

    @pl.when(pl.program_id(0) == 0)
    def _():
        column = lax.broadcasted_iota(jnp.int32, (rank, width), 1)
        fold = column % rank == lax.broadcasted_iota(jnp.int32, (rank, width), 0)
        spread = lax.dot_general(
            low[...], fold.astype(BF16), (((0,), (0,)), ((), ())), preferred_element_type=F32
        )
        place = lax.broadcasted_iota(jnp.int32, (1, width), 1) // rank
        for n in range(len(blocks)):
            mine = codes[...] == at_ref[len(blocks) + n] * most + place
            picks[n] = jnp.where(mine, spread, 0.0).astype(BF16)

    value = total[...]
    for n, block in enumerate(blocks):
        value = value + jnp.dot(picks[n], block[...], preferred_element_type=F32)
    out[...] = value


def add_expanded(order, low, codes, factors, homes, total, most):
    rank, rows = low.shape
    width = total.shape[1]
    tile = min(TILE, width)
    at = jnp.stack([jnp.asarray(x, jnp.int32) for x in [i for _, i in factors] + homes])
    full = lambda j, at: (0, 0)
    return order.call(
        functools.partial(expand_kernel, most=most, rank=rank),
        at,
        [low, codes, *[w for w, _ in factors], total],
        [pl.BlockSpec((rank, rows), full), pl.BlockSpec((rows, 1), full)]
        + [
            pl.BlockSpec((most * rank, tile), lambda j, at, n=n: (at[n], j))
            for n in range(len(factors))
        ]
        + [pl.BlockSpec((rows, tile), lambda j, at: (0, j))],
        out_shape=jax.ShapeDtypeStruct((rows, width), F32),
        grid_spec=dict(
            grid=(width // tile,),
            out_specs=pl.BlockSpec((rows, tile), lambda j, at: (0, j)),
            scratch_shapes=[pltpu.VMEM((len(factors), rows, most * rank), BF16)],
        ),
    )


def block_of(order, matrix, at, depth):
    width = matrix.shape[1]
    tile = depth // 4

    def kernel(at_ref, x, out):
        out[...] = x[...]

    return order.call(
        kernel,
        jnp.asarray(at, jnp.int32)[None],
        [matrix],
        [pl.BlockSpec((tile, width), lambda i, at: (4 * at[0] + i, 0))],
        out_shape=jax.ShapeDtypeStruct((depth, width), matrix.dtype),
        grid_spec=dict(grid=(4,), out_specs=pl.BlockSpec((tile, width), lambda i, at: (i, 0))),
    )


def shrink_kernel(at_ref, code, x, store, mates, out, held, sem, *, k, most, rank):
    for i in range(2):
        @pl.loop(0, most // 2)
        def _(j, i=i):
            j = j + i * (most // 2)
            pltpu.make_async_copy(
                store.at[at_ref[k, j]], held.at[pl.ds(j * rank, rank)], sem
            ).start()
    width = most * rank
    place = lax.broadcasted_iota(jnp.int32, (width, 1), 0) // rank
    fold = lax.broadcasted_iota(jnp.int32, (rank, width), 1) % rank == lax.broadcasted_iota(
        jnp.int32, (rank, width), 0
    )

    last = at_ref.shape[0] - 1

    def picked(block, which):
        product = lax.dot_general(
            block, x[...], (((1,), (1,)), ((), ())), preferred_element_type=F32
        )
        return jnp.where(at_ref[last, which] * most + place == code[...], product, 0.0)

    value = picked(mates[...], 1)
    pltpu.make_async_copy(held, held, sem).wait()
    out[...] = jnp.dot(
        fold.astype(F32),
        value + picked(held[...], 0),
        precision=lax.Precision.HIGHEST,
        preferred_element_type=F32,
    )


def shrink_part(order, lists, k, code, x, store, mates):
    rows, depth = code.shape[1], x.shape[1]
    most, rank = lists.shape[1], store.shape[1]
    full = lambda i, at: (0, 0)
    return order.call(
        functools.partial(shrink_kernel, k=k, most=most, rank=rank),
        lists,
        [code, x, store, mates],
        [
            pl.BlockSpec((1, rows), full),
            pl.BlockSpec((rows, depth), full),
            pl.BlockSpec(memory_space=pl.ANY),
            pl.BlockSpec((most * rank, depth), full),
        ],
        out_shape=jax.ShapeDtypeStruct((rank, rows), F32),
        grid_spec=dict(
            grid=(1,),
            out_specs=pl.BlockSpec((rank, rows), full),
            scratch_shapes=[
                pltpu.VMEM((most * rank, depth), BF16),
                pltpu.SemaphoreType.DMA(()),
            ],
        ),
    )


def body(
    tokens,
    query_base_weight,
    stored_shrink_factors,
    stored_expand_factors,
    segment_adapter,
    segment_length,
    adapter_storage_slot,
):
    groups = lax.axis_size("dp")
    lanes = lax.axis_size("tensor")
    me = lax.axis_index("dp")
    stored, rank, depth = stored_shrink_factors.shape
    used = segment_adapter.shape[1]
    most = used // 2
    rows = tokens.shape[0]
    count_all = adapter_storage_slot.shape[0]

    flat_ids = segment_adapter.reshape(-1)
    match = flat_ids[:, None] == jnp.arange(count_all, dtype=jnp.int32)[None, :]
    slot = jnp.sum(jnp.where(match, adapter_storage_slot[None, :], 0), axis=1)
    slot = slot.reshape(groups, used)
    home, local = slot // stored, slot % stored

    earlier = jnp.arange(used)[None, :] < jnp.arange(used)[:, None]
    same = home[:, :, None] == home[:, None, :]
    place = jnp.sum(jnp.where(same & earlier[None], 1, 0), axis=2)

    mine = (home == me)[:, :, None] & (place[:, :, None] == jnp.arange(most)[None, None, :])
    lists = jnp.sum(jnp.where(mine, local[:, :, None], 0), axis=1)
    to = me ^ jnp.arange(groups, dtype=jnp.int32)
    lists = jnp.sum(jnp.where((to[:, None] == jnp.arange(groups)[None])[:, :, None], lists[None], 0), axis=1)

    def send(block, k):
        return lax.ppermute(block, "dp", [(i, i ^ k) for i in range(groups)])

    here = (jnp.arange(groups) == me)[:, None]
    code_of = jnp.sum(jnp.where(here, home * most + place, 0), axis=0)
    ends = jnp.cumsum(segment_length[0])
    row_ids = jnp.arange(rows, dtype=jnp.int32)
    member = ((ends - segment_length[0])[None, :] <= row_ids[:, None]) & (
        row_ids[:, None] < ends[None, :]
    )
    code = jnp.sum(jnp.where(member, code_of[None, :], 0), axis=1)
    note = jnp.pad(code, (0, 16 * depth - rows)).reshape(16, depth).astype(BF16)
    noted = jnp.concatenate([tokens, note], axis=0)

    homes = jnp.where(jnp.arange(most) == 0, me, me ^ 1)[None]
    lists = jnp.concatenate([lists, homes])
    order = Order(lists)
    weight = query_base_weight
    line = lax.axis_index("tensor")
    shrinks, expands = stored_shrink_factors, stored_expand_factors
    across = send(noted, 2)
    plan = [[p] for p in [(0, 1), (0, 3), (1, 1), (1, 0), (1, 2), (1, 3)]]
    blocks = fetch(order, lists, [shrinks, expands], plan)
    mates = [send(x, 1) for x in blocks[:3]]
    far_b = [None, send(blocks[5], 3)]

    def shrink_of(k, code, x, mates):
        return shrink_part(order, lists, k, code[None], x, shrinks, mates)

    if lanes == 4:
        swap = [(0, 1), (1, 0), (2, 3), (3, 2)]
        middle = [(1, 2), (2, 1)]
        inward = [(0, 1), (3, 2)]
        outward = [(1, 0), (2, 3)]
        step = rows // 4
        near = lax.ppermute(tokens, "tensor", swap)
        cross = lax.ppermute(tokens, "tensor", middle)
        own = add_products(order, [([tokens], weight, line)], room=62 * 1024 * 1024)
        cross = order.hold(cross)
        out_near = lax.ppermute(cross, "tensor", outward)
        cuts = order.cut(near, [2 * step] * 2)
        far = [lax.ppermute(x, "tensor", middle) for x in cuts]
        across = order.hold(across)
        own = add_products(order, [([near], weight, line ^ 1)], own)
    part = shrink_of(0, code, tokens, mates[0])
    code_across = across[rows:].reshape(-1)[:rows].astype(F32).astype(jnp.int32)
    part = part + send(shrink_of(2, code_across, across, mates[1]), 2)
    if lanes == 4:
        far[0] = order.hold(far[0])
        out_far = [lax.ppermute(far[0], "tensor", outward)]
        far_b[1] = order.hold(far_b[1])
        part = order.hold(part)
        far_b[0] = send(order.hold(blocks[4]), 2)
        out_near = order.hold(out_near)
        part = order.hold(part + lax.ppermute(part, "tensor", inward))
        part = part + lax.ppermute(part, "tensor", middle)
        own = add_products(order, [([*far, out_near], weight, line ^ 2)], own)
        low = order.hold(part.astype(BF16))
        told = lax.ppermute(low, "tensor", outward)
        pieces = order.cut(far[1], [step] * 2)
        out_far.append(lax.ppermute(pieces[0], "tensor", outward))
        last = block_of(order, weight, line ^ 3, depth)
        told = order.hold(told)
        out_far.append(lax.ppermute(order.hold(pieces[1]), "tensor", outward))
        low = jnp.where((line == 1) | (line == 2), low, told)
    else:
        far_b[0] = send(blocks[4], 2)
        low = lax.psum(part, "tensor").astype(BF16)
    factors = [(x, 0) for x in (blocks[3], mates[2], *far_b)]
    if lanes != 4:
        whole = lax.all_gather(tokens, "tensor", axis=1, tiled=True)
        own = jnp.dot(whole, weight, preferred_element_type=F32)
    total = add_expanded(order, low, code[:, None], factors, [me ^ k for k in range(groups)], own, most)
    if lanes != 4:
        return total.astype(BF16)
    out = None
    first = 0
    for x in out_far:
        out = add_products(order, [([x, cross], last, 0)], total, first, x.shape[0], rows, out, True)
        first += x.shape[0]
    return out


def solution(mesh):
    in_specs = (
        P(("groups", "dp"), "tensor"),
        P(None, "tensor"),
        P("dp", None, "tensor"),
        P("dp", None, "tensor"),
        P("groups", None),
        P(("groups", "dp"), None),
        P("groups"),
    )
    out_specs = P(("groups", "dp"), "tensor")
    return jax.shard_map(body, mesh=mesh, in_specs=in_specs, out_specs=out_specs, check_vma=False)
```

```python
import functools

import jax
import jax.numpy as jnp
from jax import lax
from jax.experimental import pallas as pl
from jax.experimental.pallas import tpu as pltpu
from jax.sharding import PartitionSpec as P

F32 = jnp.float32
BF16 = jnp.bfloat16
ROOM = 36 * 1024 * 1024
TILE = 512


class Order:
    def __init__(self, first):
        self.last = first

    def call(self, kernel, at, args, specs, room=ROOM, **rest):
        after = [] if rest.get("input_output_aliases") else [self.last]

        def body(at_ref, *refs):
            kernel(at_ref, *refs[: len(args)], *refs[len(args) + len(after) :])

        outs = pl.pallas_call(
            body,
            grid_spec=pltpu.PrefetchScalarGridSpec(
                num_scalar_prefetch=1,
                in_specs=list(specs) + [pl.BlockSpec(memory_space=pl.ANY)] * len(after),
                **rest.pop("grid_spec"),
            ),
            compiler_params=pltpu.CompilerParams(vmem_limit_bytes=room),
            cost_estimate=pl.CostEstimate(flops=1, bytes_accessed=1, transcendentals=0),
            **rest,
        )(at, *args, *after)
        self.last = outs[0] if isinstance(outs, (list, tuple)) else outs
        return outs


    def hold(self, x):
        self.last = pl.pallas_call(
            lambda *_: None,
            out_shape=jax.ShapeDtypeStruct(x.shape, x.dtype),
            in_specs=[pl.BlockSpec(memory_space=pl.ANY)] * 2,
            out_specs=pl.BlockSpec(memory_space=pl.ANY),
            input_output_aliases={0: 0},
            cost_estimate=pl.CostEstimate(flops=1, bytes_accessed=1, transcendentals=0),
        )(x, self.last)
        return self.last


    def cut(self, x, sizes):
        def kernel(x_ref, _, *outs):
            start = 0
            for size, out in zip(sizes, outs):
                out[...] = x_ref[pl.ds(start, size)]
                start += size

        outs = pl.pallas_call(
            kernel,
            out_shape=[jax.ShapeDtypeStruct((size, x.shape[1]), x.dtype) for size in sizes],
            in_specs=[pl.BlockSpec(memory_space=pltpu.VMEM), pl.BlockSpec(memory_space=pl.ANY)],
            out_specs=[pl.BlockSpec(memory_space=pltpu.VMEM)] * len(sizes),
            compiler_params=pltpu.CompilerParams(vmem_limit_bytes=ROOM),
            cost_estimate=pl.CostEstimate(flops=1, bytes_accessed=1, transcendentals=0),
        )(x, self.last)
        self.last = outs[0]
        return outs


def fetch_kernel(lists_ref, *refs, stores, plan):
    outs, (held, in_sem, out_sem) = refs[stores:-3], refs[-3:]
    count = held.shape[1]
    steps = [(o, at, s, n) for o, pairs in enumerate(plan) for at, (s, n) in enumerate(pairs)]
    for i, (_, _, s, n) in enumerate(steps):
        @pl.loop(0, count)
        def _(j, i=i, s=s, n=n):
            pltpu.make_async_copy(
                refs[s].at[lists_ref[n, j]], held.at[i, j], in_sem.at[i]
            ).start()
    copies = []
    for i, (o, at, _, _) in enumerate(steps):
        pltpu.make_async_copy(held.at[i], held.at[i], in_sem.at[i]).wait()
        copies.append(
            pltpu.make_async_copy(
                held.at[i], outs[o].at[pl.ds(at * count, count)], out_sem.at[i]
            )
        )
        copies[-1].start()
    for copy in copies:
        copy.wait()


def fetch(order, lists, stores, plan):
    count = lists.shape[1]
    shape = stores[0].shape[1:]
    total = sum(map(len, plan))
    outs = order.call(
        functools.partial(fetch_kernel, stores=len(stores), plan=plan),
        lists,
        stores,
        [pl.BlockSpec(memory_space=pl.ANY)] * len(stores),
        out_shape=[jax.ShapeDtypeStruct((len(p) * count,) + shape, BF16) for p in plan],
        grid_spec=dict(
            grid=(1,),
            out_specs=[pl.BlockSpec(memory_space=pl.ANY)] * len(plan),
            scratch_shapes=[
                pltpu.VMEM((total, count) + shape, BF16),
                pltpu.SemaphoreType.DMA((total,)),
                pltpu.SemaphoreType.DMA((total,)),
            ],
        ),
    )
    return [o.reshape(o.shape[0] * shape[0], shape[1]) for o in outs]


def sum_kernel(at_ref, *refs, plan, has_total, has_out, rounded):
    refs = list(refs)
    factors = [([refs.pop(0) for _ in range(n)], refs.pop(0)) for n in plan]
    total = refs.pop(0) if has_total else None
    if has_out:
        refs.pop(0)
    out = refs.pop(0)
    value = total[...] if has_total else None
    for xs, w in factors:
        if len(xs) > 1:
            both = refs.pop(0)

            @pl.when(pl.program_id(0) == 0)
            def _(xs=xs, both=both):
                start = 0
                for x in xs[:-1]:
                    part = pl.ds(start, x.shape[0])
                    both[part] = x[...] + xs[-1][part]
                    start += x.shape[0]

            x = both
        else:
            x = xs[0]
        product = jnp.dot(x[...], w[...], preferred_element_type=F32)
        value = product if value is None else value + product
    out[...] = value.astype(BF16) if rounded else value


def add_products(order, terms, total=None, first=0, rows=None, whole=None, out=None, rounded=False, room=ROOM):
    rows = rows or terms[0][0][-1].shape[0]
    width = terms[0][1].shape[1]
    tile = min(4 * TILE if rounded and rows <= 192 else 2 * TILE if rounded else TILE, width)
    at = jnp.stack([jnp.asarray(t[2], jnp.int32) for t in terms])
    here = first // rows
    there = here if whole else 0
    specs, args, scratch = [], [], []
    for n, (xs, w, _) in enumerate(terms):
        depth = xs[0].shape[1]
        for x in xs:
            at_row = here if x is xs[-1] and x.shape[0] > rows else 0
            specs.append(
                pl.BlockSpec((min(rows, x.shape[0]), depth), lambda j, at, i=at_row: (i, 0))
            )
            args.append(x)
        specs.append(pl.BlockSpec((depth, tile), lambda j, at, n=n: (at[n], j)))
        args.append(w)
        if len(xs) > 1:
            scratch.append(pltpu.VMEM((rows, depth), BF16))
    if total is not None:
        specs.append(pl.BlockSpec((rows, tile), lambda j, at: (here, j)))
        args.append(total)
    aliases = {}
    if out is not None:
        aliases = {len(args) + 1: 0}
        specs.append(pl.BlockSpec(memory_space=pl.ANY))
        args.append(out)
    dtype = BF16 if rounded else F32
    return order.call(
        functools.partial(
            sum_kernel,
            plan=[len(t[0]) for t in terms],
            has_total=total is not None,
            has_out=out is not None,
            rounded=rounded,
        ),
        at,
        args,
        specs,
        room,
        out_shape=jax.ShapeDtypeStruct((whole or rows, width), dtype),
        grid_spec=dict(
            grid=(width // tile,),
            out_specs=pl.BlockSpec((rows, tile), lambda j, at: (there, j)),
            scratch_shapes=scratch,
        ),
        input_output_aliases=aliases,
    )


def expand_kernel(at_ref, low, codes, *refs, most, rank):
    blocks, (total, out, picks) = refs[:-3], refs[-3:]
    width = most * rank

    @pl.when(pl.program_id(0) == 0)
    def _():
        column = lax.broadcasted_iota(jnp.int32, (rank, width), 1)
        fold = column % rank == lax.broadcasted_iota(jnp.int32, (rank, width), 0)
        spread = lax.dot_general(
            low[...], fold.astype(BF16), (((0,), (0,)), ((), ())), preferred_element_type=F32
        )
        place = lax.broadcasted_iota(jnp.int32, (1, width), 1) // rank
        for n in range(len(blocks)):
            mine = codes[...] == at_ref[len(blocks) + n] * most + place
            picks[n] = jnp.where(mine, spread, 0.0).astype(BF16)

    value = total[...]
    for n, block in enumerate(blocks):
        value = value + jnp.dot(picks[n], block[...], preferred_element_type=F32)
    out[...] = value


def add_expanded(order, low, codes, factors, homes, total, most):
    rank, rows = low.shape
    width = total.shape[1]
    tile = min(TILE, width)
    at = jnp.stack([jnp.asarray(x, jnp.int32) for x in [i for _, i in factors] + homes])
    full = lambda j, at: (0, 0)
    return order.call(
        functools.partial(expand_kernel, most=most, rank=rank),
        at,
        [low, codes, *[w for w, _ in factors], total],
        [pl.BlockSpec((rank, rows), full), pl.BlockSpec((rows, 1), full)]
        + [
            pl.BlockSpec((most * rank, tile), lambda j, at, n=n: (at[n], j))
            for n in range(len(factors))
        ]
        + [pl.BlockSpec((rows, tile), lambda j, at: (0, j))],
        out_shape=jax.ShapeDtypeStruct((rows, width), F32),
        grid_spec=dict(
            grid=(width // tile,),
            out_specs=pl.BlockSpec((rows, tile), lambda j, at: (0, j)),
            scratch_shapes=[pltpu.VMEM((len(factors), rows, most * rank), BF16)],
        ),
    )


def block_of(order, matrix, at, depth):
    width = matrix.shape[1]
    tile = depth // 4

    def kernel(at_ref, x, out):
        out[...] = x[...]

    return order.call(
        kernel,
        jnp.asarray(at, jnp.int32)[None],
        [matrix],
        [pl.BlockSpec((tile, width), lambda i, at: (4 * at[0] + i, 0))],
        out_shape=jax.ShapeDtypeStruct((depth, width), matrix.dtype),
        grid_spec=dict(grid=(4,), out_specs=pl.BlockSpec((tile, width), lambda i, at: (i, 0))),
    )


def shrink_kernel(at_ref, code, x, store, mates, out, held, sem, *, k, most, rank):
    for i in range(2):
        @pl.loop(0, most // 2)
        def _(j, i=i):
            j = j + i * (most // 2)
            pltpu.make_async_copy(
                store.at[at_ref[k, j]], held.at[pl.ds(j * rank, rank)], sem
            ).start()
    width = most * rank
    place = lax.broadcasted_iota(jnp.int32, (width, 1), 0) // rank
    fold = lax.broadcasted_iota(jnp.int32, (rank, width), 1) % rank == lax.broadcasted_iota(
        jnp.int32, (rank, width), 0
    )

    last = at_ref.shape[0] - 1

    def picked(block, which):
        product = lax.dot_general(
            block, x[...], (((1,), (1,)), ((), ())), preferred_element_type=F32
        )
        return jnp.where(at_ref[last, which] * most + place == code[...], product, 0.0)

    value = picked(mates[...], 1)
    pltpu.make_async_copy(held, held, sem).wait()
    out[...] = jnp.dot(
        fold.astype(F32),
        value + picked(held[...], 0),
        precision=lax.Precision.HIGHEST,
        preferred_element_type=F32,
    )


def shrink_part(order, lists, k, code, x, store, mates):
    rows, depth = code.shape[1], x.shape[1]
    most, rank = lists.shape[1], store.shape[1]
    full = lambda i, at: (0, 0)
    return order.call(
        functools.partial(shrink_kernel, k=k, most=most, rank=rank),
        lists,
        [code, x, store, mates],
        [
            pl.BlockSpec((1, rows), full),
            pl.BlockSpec((rows, depth), full),
            pl.BlockSpec(memory_space=pl.ANY),
            pl.BlockSpec((most * rank, depth), full),
        ],
        out_shape=jax.ShapeDtypeStruct((rank, rows), F32),
        grid_spec=dict(
            grid=(1,),
            out_specs=pl.BlockSpec((rank, rows), full),
            scratch_shapes=[
                pltpu.VMEM((most * rank, depth), BF16),
                pltpu.SemaphoreType.DMA(()),
            ],
        ),
    )


def body(
    tokens,
    query_base_weight,
    stored_shrink_factors,
    stored_expand_factors,
    segment_adapter,
    segment_length,
    adapter_storage_slot,
):
    groups = lax.axis_size("dp")
    lanes = lax.axis_size("tensor")
    me = lax.axis_index("dp")
    stored, rank, depth = stored_shrink_factors.shape
    used = segment_adapter.shape[1]
    most = used // 2
    rows = tokens.shape[0]
    count_all = adapter_storage_slot.shape[0]

    flat_ids = segment_adapter.reshape(-1)
    match = flat_ids[:, None] == jnp.arange(count_all, dtype=jnp.int32)[None, :]
    slot = jnp.sum(jnp.where(match, adapter_storage_slot[None, :], 0), axis=1)
    slot = slot.reshape(groups, used)
    home, local = slot // stored, slot % stored

    earlier = jnp.arange(used)[None, :] < jnp.arange(used)[:, None]
    same = home[:, :, None] == home[:, None, :]
    place = jnp.sum(jnp.where(same & earlier[None], 1, 0), axis=2)

    mine = (home == me)[:, :, None] & (place[:, :, None] == jnp.arange(most)[None, None, :])
    lists = jnp.sum(jnp.where(mine, local[:, :, None], 0), axis=1)
    to = me ^ jnp.arange(groups, dtype=jnp.int32)
    lists = jnp.sum(jnp.where((to[:, None] == jnp.arange(groups)[None])[:, :, None], lists[None], 0), axis=1)

    def send(block, k):
        return lax.ppermute(block, "dp", [(i, i ^ k) for i in range(groups)])

    here = (jnp.arange(groups) == me)[:, None]
    code_of = jnp.sum(jnp.where(here, home * most + place, 0), axis=0)
    ends = jnp.cumsum(segment_length[0])
    row_ids = jnp.arange(rows, dtype=jnp.int32)
    member = ((ends - segment_length[0])[None, :] <= row_ids[:, None]) & (
        row_ids[:, None] < ends[None, :]
    )
    code = jnp.sum(jnp.where(member, code_of[None, :], 0), axis=1)
    note = jnp.pad(code, (0, 16 * depth - rows)).reshape(16, depth).astype(BF16)
    noted = jnp.concatenate([tokens, note], axis=0)

    homes = jnp.where(jnp.arange(most) == 0, me, me ^ 1)[None]
    lists = jnp.concatenate([lists, homes])
    order = Order(lists)
    weight = query_base_weight
    line = lax.axis_index("tensor")
    shrinks, expands = stored_shrink_factors, stored_expand_factors
    across = send(noted, 2)
    if lanes == 4:
        own = add_products(order, [([tokens], weight, line)], room=62 * 1024 * 1024)
    plan = [[p] for p in [(0, 1), (0, 3), (1, 1), (1, 0), (1, 2), (1, 3)]]
    blocks = fetch(order, lists, [shrinks, expands], plan)
    mates = [send(x, 1) for x in blocks[:3]]
    far_b = [None, send(blocks[5], 3)]

    def shrink_of(k, code, x, mates):
        return shrink_part(order, lists, k, code[None], x, shrinks, mates)

    if lanes == 4:
        swap = [(0, 1), (1, 0), (2, 3), (3, 2)]
        middle = [(1, 2), (2, 1)]
        inward = [(0, 1), (3, 2)]
        outward = [(1, 0), (2, 3)]
        step = rows // 4
        near = lax.ppermute(tokens, "tensor", swap)
        cross = lax.ppermute(tokens, "tensor", middle)
        cross = order.hold(cross)
        out_near = lax.ppermute(cross, "tensor", outward)
        cuts = order.cut(near, [2 * step] * 2)
        far = [lax.ppermute(x, "tensor", middle) for x in cuts]
        across = order.hold(across)
        own = add_products(order, [([near], weight, line ^ 1)], own)
    part = shrink_of(0, code, tokens, mates[0])
    code_across = across[rows:].reshape(-1)[:rows].astype(F32).astype(jnp.int32)
    part = part + send(shrink_of(2, code_across, across, mates[1]), 2)
    if lanes == 4:
        far[0] = order.hold(far[0])
        out_far = [lax.ppermute(far[0], "tensor", outward)]
        far_b[1] = order.hold(far_b[1])
        part = order.hold(part)
        far_b[0] = send(order.hold(blocks[4]), 2)
        out_near = order.hold(out_near)
        part = order.hold(part + lax.ppermute(part, "tensor", inward))
        part = part + lax.ppermute(part, "tensor", middle)
        own = add_products(order, [([*far, out_near], weight, line ^ 2)], own)
        low = order.hold(part.astype(BF16))
        told = lax.ppermute(low, "tensor", outward)
        pieces = order.cut(far[1], [step] * 2)
        out_far.append(lax.ppermute(pieces[0], "tensor", outward))
        last = block_of(order, weight, line ^ 3, depth)
        told = order.hold(told)
        out_far.append(lax.ppermute(order.hold(pieces[1]), "tensor", outward))
        low = jnp.where((line == 1) | (line == 2), low, told)
    else:
        far_b[0] = send(blocks[4], 2)
        low = lax.psum(part, "tensor").astype(BF16)
    factors = [(x, 0) for x in (blocks[3], mates[2], *far_b)]
    if lanes != 4:
        whole = lax.all_gather(tokens, "tensor", axis=1, tiled=True)
        own = jnp.dot(whole, weight, preferred_element_type=F32)
    total = add_expanded(order, low, code[:, None], factors, [me ^ k for k in range(groups)], own, most)
    if lanes != 4:
        return total.astype(BF16)
    out = None
    first = 0
    for x in out_far:
        out = add_products(order, [([x, cross], last, 0)], total, first, x.shape[0], rows, out, True)
        first += x.shape[0]
    return out


def solution(mesh):
    in_specs = (
        P(("groups", "dp"), "tensor"),
        P(None, "tensor"),
        P("dp", None, "tensor"),
        P("dp", None, "tensor"),
        P("groups", None),
        P(("groups", "dp"), None),
        P("groups"),
    )
    out_specs = P(("groups", "dp"), "tensor")
    return jax.shard_map(body, mesh=mesh, in_specs=in_specs, out_specs=out_specs, check_vma=False)
```

```python
import functools

import jax
import jax.numpy as jnp
from jax import lax
from jax.experimental import pallas as pl
from jax.experimental.pallas import tpu as pltpu
from jax.sharding import PartitionSpec as P

F32 = jnp.float32
BF16 = jnp.bfloat16
ROOM = 36 * 1024 * 1024
TILE = 512


class Order:
    def __init__(self, first):
        self.last = first

    def call(self, kernel, at, args, specs, room=ROOM, **rest):
        after = [] if rest.get("input_output_aliases") else [self.last]

        def body(at_ref, *refs):
            kernel(at_ref, *refs[: len(args)], *refs[len(args) + len(after) :])

        outs = pl.pallas_call(
            body,
            grid_spec=pltpu.PrefetchScalarGridSpec(
                num_scalar_prefetch=1,
                in_specs=list(specs) + [pl.BlockSpec(memory_space=pl.ANY)] * len(after),
                **rest.pop("grid_spec"),
            ),
            compiler_params=pltpu.CompilerParams(vmem_limit_bytes=room),
            cost_estimate=pl.CostEstimate(flops=1, bytes_accessed=1, transcendentals=0),
            **rest,
        )(at, *args, *after)
        self.last = outs[0] if isinstance(outs, (list, tuple)) else outs
        return outs


    def hold(self, x):
        self.last = pl.pallas_call(
            lambda *_: None,
            out_shape=jax.ShapeDtypeStruct(x.shape, x.dtype),
            in_specs=[pl.BlockSpec(memory_space=pl.ANY)] * 2,
            out_specs=pl.BlockSpec(memory_space=pl.ANY),
            input_output_aliases={0: 0},
            cost_estimate=pl.CostEstimate(flops=1, bytes_accessed=1, transcendentals=0),
        )(x, self.last)
        return self.last


    def cut(self, x, sizes):
        def kernel(x_ref, _, *outs):
            start = 0
            for size, out in zip(sizes, outs):
                out[...] = x_ref[pl.ds(start, size)]
                start += size

        outs = pl.pallas_call(
            kernel,
            out_shape=[jax.ShapeDtypeStruct((size, x.shape[1]), x.dtype) for size in sizes],
            in_specs=[pl.BlockSpec(memory_space=pltpu.VMEM), pl.BlockSpec(memory_space=pl.ANY)],
            out_specs=[pl.BlockSpec(memory_space=pltpu.VMEM)] * len(sizes),
            compiler_params=pltpu.CompilerParams(vmem_limit_bytes=ROOM),
            cost_estimate=pl.CostEstimate(flops=1, bytes_accessed=1, transcendentals=0),
        )(x, self.last)
        self.last = outs[0]
        return outs


def fetch_kernel(lists_ref, *refs, stores, plan):
    outs, (held, in_sem, out_sem) = refs[stores:-3], refs[-3:]
    count = held.shape[1]
    steps = [(o, at, s, n) for o, pairs in enumerate(plan) for at, (s, n) in enumerate(pairs)]
    for i, (_, _, s, n) in enumerate(steps):
        @pl.loop(0, count)
        def _(j, i=i, s=s, n=n):
            pltpu.make_async_copy(
                refs[s].at[lists_ref[n, j]], held.at[i, j], in_sem.at[i]
            ).start()
    copies = []
    for i, (o, at, _, _) in enumerate(steps):
        pltpu.make_async_copy(held.at[i], held.at[i], in_sem.at[i]).wait()
        copies.append(
            pltpu.make_async_copy(
                held.at[i], outs[o].at[pl.ds(at * count, count)], out_sem.at[i]
            )
        )
        copies[-1].start()
    for copy in copies:
        copy.wait()


def fetch(order, lists, stores, plan):
    count = lists.shape[1]
    shape = stores[0].shape[1:]
    total = sum(map(len, plan))
    outs = order.call(
        functools.partial(fetch_kernel, stores=len(stores), plan=plan),
        lists,
        stores,
        [pl.BlockSpec(memory_space=pl.ANY)] * len(stores),
        out_shape=[jax.ShapeDtypeStruct((len(p) * count,) + shape, BF16) for p in plan],
        grid_spec=dict(
            grid=(1,),
            out_specs=[pl.BlockSpec(memory_space=pl.ANY)] * len(plan),
            scratch_shapes=[
                pltpu.VMEM((total, count) + shape, BF16),
                pltpu.SemaphoreType.DMA((total,)),
                pltpu.SemaphoreType.DMA((total,)),
            ],
        ),
    )
    return [o.reshape(o.shape[0] * shape[0], shape[1]) for o in outs]


def sum_kernel(at_ref, *refs, plan, has_total, has_out, rounded):
    refs = list(refs)
    factors = [([refs.pop(0) for _ in range(n)], refs.pop(0)) for n in plan]
    total = refs.pop(0) if has_total else None
    if has_out:
        refs.pop(0)
    out = refs.pop(0)
    value = total[...] if has_total else None
    for xs, w in factors:
        if len(xs) > 1:
            both = refs.pop(0)

            @pl.when(pl.program_id(0) == 0)
            def _(xs=xs, both=both):
                start = 0
                for x in xs[:-1]:
                    part = pl.ds(start, x.shape[0])
                    both[part] = x[...] + xs[-1][part]
                    start += x.shape[0]

            x = both
        else:
            x = xs[0]
        product = jnp.dot(x[...], w[...], preferred_element_type=F32)
        value = product if value is None else value + product
    out[...] = value.astype(BF16) if rounded else value


def add_products(order, terms, total=None, first=0, rows=None, whole=None, out=None, rounded=False, room=ROOM):
    rows = rows or terms[0][0][-1].shape[0]
    width = terms[0][1].shape[1]
    tile = min(4 * TILE if rounded and rows <= 192 else 2 * TILE if rounded else TILE, width)
    at = jnp.stack([jnp.asarray(t[2], jnp.int32) for t in terms])
    here = first // rows
    there = here if whole else 0
    specs, args, scratch = [], [], []
    for n, (xs, w, _) in enumerate(terms):
        depth = xs[0].shape[1]
        for x in xs:
            at_row = here if x is xs[-1] and x.shape[0] > rows else 0
            specs.append(
                pl.BlockSpec((min(rows, x.shape[0]), depth), lambda j, at, i=at_row: (i, 0))
            )
            args.append(x)
        specs.append(pl.BlockSpec((depth, tile), lambda j, at, n=n: (at[n], j)))
        args.append(w)
        if len(xs) > 1:
            scratch.append(pltpu.VMEM((rows, depth), BF16))
    if total is not None:
        specs.append(pl.BlockSpec((rows, tile), lambda j, at: (here, j)))
        args.append(total)
    aliases = {}
    if out is not None:
        aliases = {len(args) + 1: 0}
        specs.append(pl.BlockSpec(memory_space=pl.ANY))
        args.append(out)
    dtype = BF16 if rounded else F32
    return order.call(
        functools.partial(
            sum_kernel,
            plan=[len(t[0]) for t in terms],
            has_total=total is not None,
            has_out=out is not None,
            rounded=rounded,
        ),
        at,
        args,
        specs,
        room,
        out_shape=jax.ShapeDtypeStruct((whole or rows, width), dtype),
        grid_spec=dict(
            grid=(width // tile,),
            out_specs=pl.BlockSpec((rows, tile), lambda j, at: (there, j)),
            scratch_shapes=scratch,
        ),
        input_output_aliases=aliases,
    )


def expand_kernel(at_ref, low, codes, *refs, most, rank):
    blocks, (total, out, picks) = refs[:-3], refs[-3:]
    width = most * rank

    @pl.when(pl.program_id(0) == 0)
    def _():
        column = lax.broadcasted_iota(jnp.int32, (rank, width), 1)
        fold = column % rank == lax.broadcasted_iota(jnp.int32, (rank, width), 0)
        spread = lax.dot_general(
            low[...], fold.astype(BF16), (((0,), (0,)), ((), ())), preferred_element_type=F32
        )
        place = lax.broadcasted_iota(jnp.int32, (1, width), 1) // rank
        for n in range(len(blocks)):
            mine = codes[...] == at_ref[len(blocks) + n] * most + place
            picks[n] = jnp.where(mine, spread, 0.0).astype(BF16)

    value = total[...]
    for n, block in enumerate(blocks):
        value = value + jnp.dot(picks[n], block[...], preferred_element_type=F32)
    out[...] = value


def add_expanded(order, low, codes, factors, homes, total, most):
    rank, rows = low.shape
    width = total.shape[1]
    tile = min(2 * TILE, width)
    at = jnp.stack([jnp.asarray(x, jnp.int32) for x in [i for _, i in factors] + homes])
    full = lambda j, at: (0, 0)
    return order.call(
        functools.partial(expand_kernel, most=most, rank=rank),
        at,
        [low, codes, *[w for w, _ in factors], total],
        [pl.BlockSpec((rank, rows), full), pl.BlockSpec((rows, 1), full)]
        + [
            pl.BlockSpec((most * rank, tile), lambda j, at, n=n: (at[n], j))
            for n in range(len(factors))
        ]
        + [pl.BlockSpec((rows, tile), lambda j, at: (0, j))],
        out_shape=jax.ShapeDtypeStruct((rows, width), F32),
        grid_spec=dict(
            grid=(width // tile,),
            out_specs=pl.BlockSpec((rows, tile), lambda j, at: (0, j)),
            scratch_shapes=[pltpu.VMEM((len(factors), rows, most * rank), BF16)],
        ),
    )


def block_of(order, matrix, at, depth):
    width = matrix.shape[1]
    tile = depth // 4

    def kernel(at_ref, x, out):
        out[...] = x[...]

    return order.call(
        kernel,
        jnp.asarray(at, jnp.int32)[None],
        [matrix],
        [pl.BlockSpec((tile, width), lambda i, at: (4 * at[0] + i, 0))],
        out_shape=jax.ShapeDtypeStruct((depth, width), matrix.dtype),
        grid_spec=dict(grid=(4,), out_specs=pl.BlockSpec((tile, width), lambda i, at: (i, 0))),
    )


def shrink_kernel(at_ref, code, x, store, mates, out, held, sem, *, k, most, rank):
    for i in range(2):
        @pl.loop(0, most // 2)
        def _(j, i=i):
            j = j + i * (most // 2)
            pltpu.make_async_copy(
                store.at[at_ref[k, j]], held.at[pl.ds(j * rank, rank)], sem
            ).start()
    width = most * rank
    place = lax.broadcasted_iota(jnp.int32, (width, 1), 0) // rank
    fold = lax.broadcasted_iota(jnp.int32, (rank, width), 1) % rank == lax.broadcasted_iota(
        jnp.int32, (rank, width), 0
    )

    last = at_ref.shape[0] - 1

    def picked(block, which):
        product = lax.dot_general(
            block, x[...], (((1,), (1,)), ((), ())), preferred_element_type=F32
        )
        return jnp.where(at_ref[last, which] * most + place == code[...], product, 0.0)

    value = picked(mates[...], 1)
    pltpu.make_async_copy(held, held, sem).wait()
    out[...] = jnp.dot(
        fold.astype(F32),
        value + picked(held[...], 0),
        precision=lax.Precision.HIGHEST,
        preferred_element_type=F32,
    )


def shrink_part(order, lists, k, code, x, store, mates):
    rows, depth = code.shape[1], x.shape[1]
    most, rank = lists.shape[1], store.shape[1]
    full = lambda i, at: (0, 0)
    return order.call(
        functools.partial(shrink_kernel, k=k, most=most, rank=rank),
        lists,
        [code, x, store, mates],
        [
            pl.BlockSpec((1, rows), full),
            pl.BlockSpec((rows, depth), full),
            pl.BlockSpec(memory_space=pl.ANY),
            pl.BlockSpec((most * rank, depth), full),
        ],
        out_shape=jax.ShapeDtypeStruct((rank, rows), F32),
        grid_spec=dict(
            grid=(1,),
            out_specs=pl.BlockSpec((rank, rows), full),
            scratch_shapes=[
                pltpu.VMEM((most * rank, depth), BF16),
                pltpu.SemaphoreType.DMA(()),
            ],
        ),
    )


def body(
    tokens,
    query_base_weight,
    stored_shrink_factors,
    stored_expand_factors,
    segment_adapter,
    segment_length,
    adapter_storage_slot,
):
    groups = lax.axis_size("dp")
    lanes = lax.axis_size("tensor")
    me = lax.axis_index("dp")
    stored, rank, depth = stored_shrink_factors.shape
    used = segment_adapter.shape[1]
    most = used // 2
    rows = tokens.shape[0]
    count_all = adapter_storage_slot.shape[0]

    flat_ids = segment_adapter.reshape(-1)
    match = flat_ids[:, None] == jnp.arange(count_all, dtype=jnp.int32)[None, :]
    slot = jnp.sum(jnp.where(match, adapter_storage_slot[None, :], 0), axis=1)
    slot = slot.reshape(groups, used)
    home, local = slot // stored, slot % stored

    earlier = jnp.arange(used)[None, :] < jnp.arange(used)[:, None]
    same = home[:, :, None] == home[:, None, :]
    place = jnp.sum(jnp.where(same & earlier[None], 1, 0), axis=2)

    mine = (home == me)[:, :, None] & (place[:, :, None] == jnp.arange(most)[None, None, :])
    lists = jnp.sum(jnp.where(mine, local[:, :, None], 0), axis=1)
    to = me ^ jnp.arange(groups, dtype=jnp.int32)
    lists = jnp.sum(jnp.where((to[:, None] == jnp.arange(groups)[None])[:, :, None], lists[None], 0), axis=1)

    def send(block, k):
        return lax.ppermute(block, "dp", [(i, i ^ k) for i in range(groups)])

    here = (jnp.arange(groups) == me)[:, None]
    code_of = jnp.sum(jnp.where(here, home * most + place, 0), axis=0)
    ends = jnp.cumsum(segment_length[0])
    row_ids = jnp.arange(rows, dtype=jnp.int32)
    member = ((ends - segment_length[0])[None, :] <= row_ids[:, None]) & (
        row_ids[:, None] < ends[None, :]
    )
    code = jnp.sum(jnp.where(member, code_of[None, :], 0), axis=1)
    note = jnp.pad(code, (0, 16 * depth - rows)).reshape(16, depth).astype(BF16)
    noted = jnp.concatenate([tokens, note], axis=0)

    homes = jnp.where(jnp.arange(most) == 0, me, me ^ 1)[None]
    lists = jnp.concatenate([lists, homes])
    order = Order(lists)
    weight = query_base_weight
    line = lax.axis_index("tensor")
    shrinks, expands = stored_shrink_factors, stored_expand_factors
    across = send(noted, 2)
    if lanes == 4:
        own = add_products(order, [([tokens], weight, line)], room=62 * 1024 * 1024)
    plan = [[p] for p in [(0, 1), (0, 3), (1, 1), (1, 0), (1, 2), (1, 3)]]
    blocks = fetch(order, lists, [shrinks, expands], plan)
    mates = [send(x, 1) for x in blocks[:3]]
    far_b = [None, send(blocks[5], 3)]

    def shrink_of(k, code, x, mates):
        return shrink_part(order, lists, k, code[None], x, shrinks, mates)

    if lanes == 4:
        swap = [(0, 1), (1, 0), (2, 3), (3, 2)]
        middle = [(1, 2), (2, 1)]
        inward = [(0, 1), (3, 2)]
        outward = [(1, 0), (2, 3)]
        step = rows // 4
        near = lax.ppermute(tokens, "tensor", swap)
        cross = lax.ppermute(tokens, "tensor", middle)
        cross = order.hold(cross)
        out_near = lax.ppermute(cross, "tensor", outward)
        cuts = order.cut(near, [2 * step] * 2)
        far = [lax.ppermute(x, "tensor", middle) for x in cuts]
        across = order.hold(across)
        own = add_products(order, [([near], weight, line ^ 1)], own)
    part = shrink_of(0, code, tokens, mates[0])
    code_across = across[rows:].reshape(-1)[:rows].astype(F32).astype(jnp.int32)
    part = part + send(shrink_of(2, code_across, across, mates[1]), 2)
    if lanes == 4:
        far[0] = order.hold(far[0])
        out_far = [lax.ppermute(far[0], "tensor", outward)]
        far_b[1] = order.hold(far_b[1])
        part = order.hold(part)
        far_b[0] = send(order.hold(blocks[4]), 2)
        out_near = order.hold(out_near)
        part = order.hold(part + lax.ppermute(part, "tensor", inward))
        part = part + lax.ppermute(part, "tensor", middle)
        own = add_products(order, [([*far, out_near], weight, line ^ 2)], own)
        low = order.hold(part.astype(BF16))
        told = lax.ppermute(low, "tensor", outward)
        pieces = order.cut(far[1], [step] * 2)
        out_far.append(lax.ppermute(pieces[0], "tensor", outward))
        last = block_of(order, weight, line ^ 3, depth)
        told = order.hold(told)
        out_far.append(lax.ppermute(order.hold(pieces[1]), "tensor", outward))
        low = jnp.where((line == 1) | (line == 2), low, told)
    else:
        far_b[0] = send(blocks[4], 2)
        low = lax.psum(part, "tensor").astype(BF16)
    factors = [(x, 0) for x in (blocks[3], mates[2], *far_b)]
    if lanes != 4:
        whole = lax.all_gather(tokens, "tensor", axis=1, tiled=True)
        own = jnp.dot(whole, weight, preferred_element_type=F32)
    total = add_expanded(order, low, code[:, None], factors, [me ^ k for k in range(groups)], own, most)
    if lanes != 4:
        return total.astype(BF16)
    out = None
    first = 0
    for x in out_far:
        out = add_products(order, [([x, cross], last, 0)], total, first, x.shape[0], rows, out, True)
        first += x.shape[0]
    return out


def solution(mesh):
    in_specs = (
        P(("groups", "dp"), "tensor"),
        P(None, "tensor"),
        P("dp", None, "tensor"),
        P("dp", None, "tensor"),
        P("groups", None),
        P(("groups", "dp"), None),
        P("groups"),
    )
    out_specs = P(("groups", "dp"), "tensor")
    return jax.shard_map(body, mesh=mesh, in_specs=in_specs, out_specs=out_specs, check_vma=False)
```
